256 devices in a mesh: sub: 2 (over z_hi), row: 8 (over x, core), col: 16 (over z_lo, y).
Axes of the slice: x: 4, y: 4, z: 8 (z_hi: 2, z_lo: 4; z = z_hi * 4 + z_lo), core: 2. Of those that a mesh axis runs over, the one named last changes fastest.
Arguments:
- panel: float32 [65536, 512], P(('sub', 'row', 'col')), as said below
- trailing: float32 [65536, 4096], P(('sub', 'row'), 'col'), may hold values from -6 to 6
- child: float32 [2, 16384, 4096], P('sub', 'row', 'col'), may hold values from -6 to 6
- child_map: int32 [2, 64], P('sub', 'row'), may hold values from 0 to 31, as said below
- pattern: int32 [256, 16], P(('sub', 'row'), 'col'), may hold values from 0 to 1
Outputs:
- factor: float32 [65536, 512], P(('sub', 'row', 'col'))
- updated: float32 [65536, 4096], P(('sub', 'row'), 'col')
The draws below stay inside these ranges and needn't reach their ends.
Inputs may be any that keep to these rules, and one draw needn't show every extreme that they name: `child_map`: the child block rows held by one index of row map to distinct slots; slot v means half v // 16 of sub and block v % 16 of that row index's block rows. The last entry of each such run of 8 is 16 * 2 - 1. `panel`: rows 0 to 511 form a symmetric positive definite block.
All inputs are finite; a program needn't handle non-finite values.
Results may differ from the reference program's by a relative error of at most 0.00007.
Values sent between devices are 32-bit elements; how exact they have to be, the bound alone decides.
No kernel may reach another device: no remote copies, remote signals or barrier semaphores. Data moves between devices by JAX's collectives and lax.ppermute only.
A program may use at most 128 MiB of HBM per device.

```python
import jax
import jax.numpy as jnp
from jax import lax

NF = 65536
B = 256
P_SIZE = 512
CBD = 8
SUBS = 2
FB = 256
RBD = 16
WT = 4096
CH_BLOCKS = 64
N_SUB = 2
N_ROW = 8
N_COL = 16


def draw_panel(key, part):
    key_diag = jax.random.fold_in(key, 11)
    key_off = jax.random.fold_in(key, 12)
    key_rest = jax.random.fold_in(key, 13)
    diagonal_part = jax.random.uniform(key_diag, (P_SIZE,), jnp.float32, 1.7, 3.0)
    uniform_off = jax.random.uniform(key_off, (P_SIZE, P_SIZE), jnp.float32, -1.0, 1.0)
    symmetric_off = (uniform_off + uniform_off.T) * (0.8 / P_SIZE)
    is_diagonal = jnp.arange(P_SIZE)[:, None] == jnp.arange(P_SIZE)[None, :]
    pivot_top = jnp.where(is_diagonal, diagonal_part[:, None] + jnp.zeros((P_SIZE, P_SIZE), jnp.float32), symmetric_off)
    lower_rows = 0.3 * jax.random.normal(key_rest, (NF - P_SIZE, P_SIZE), jnp.float32)
    return jnp.concatenate([pivot_top, lower_rows], axis=0).astype(jnp.float32)


def draw_child_map(key, part):
    groups = SUBS * N_ROW
    key_list = jax.random.split(jax.random.fold_in(key, 21), groups)
    slot_total = N_SUB * RBD
    shuffled = jax.vmap(lambda single: jax.random.permutation(single, slot_total - 1))(key_list)
    chosen = shuffled[:, :CBD - 1].astype(jnp.int32)
    last_slot = jnp.full((groups, 1), slot_total - 1, jnp.int32)
    return jnp.concatenate([chosen, last_slot], axis=1).reshape(SUBS, CBD * N_ROW).astype(jnp.int32)


def draw_pattern(key, part):
    values = jax.random.randint(jax.random.fold_in(key, 31), (FB, N_COL), 0, 4)
    block_rows = jnp.arange(FB, dtype=jnp.int32)[:, None]
    threshold = jnp.where(block_rows < FB // 4, 3, 1)
    return (values < threshold).astype(jnp.int32)


def levels(key, extent, pieces, least, largest):
    loudness = 1.0
    for dim, parts in pieces:
        heights = jax.random.uniform(jax.random.fold_in(jax.random.fold_in(key, 6), dim), (parts,), jnp.float32, least / len(pieces), largest / len(pieces))
        loudness = loudness * jnp.repeat(jnp.exp(heights), extent[dim] // parts).reshape((-1,) + (1,) * (len(extent) - 1 - dim))
    return loudness


def centred(own_key, shape, spread, bound, cuts=(), held_as=jnp.bfloat16):
    gain = levels(own_key, shape, cuts, -0.22, 0.18) if cuts else 1.0
    drawn = jax.random.normal(own_key, shape, jnp.float32) * spread * gain
    return jnp.minimum(jnp.maximum(drawn, -bound), bound).astype(held_as)


def setup_inputs(seed: int = 0) -> dict:
    keys = jax.random.split(jax.random.key(seed), 6)
    panel = draw_panel(jax.random.fold_in(keys[5], 71), 0)
    trailing = centred(keys[1], (NF, WT), 1.0, 6.0, ((0, 16), (1, 16)), jnp.float32)
    child = centred(keys[2], (SUBS, CH_BLOCKS * B, WT), 1.0, 6.0, ((0, 2), (1, 8), (2, 16)), jnp.float32)
    child_map = draw_child_map(jax.random.fold_in(keys[5], 71), 0)
    pattern = draw_pattern(jax.random.fold_in(keys[5], 71), 0)
    return {"panel": panel, "trailing": trailing, "child": child, "child_map": child_map, "pattern": pattern}


def reference(panel, trailing, child, child_map, pattern):
    pivot_top = panel[:P_SIZE]
    lower_factor = jnp.linalg.cholesky(pivot_top)
    identity = jnp.eye(P_SIZE, dtype=panel.dtype)
    inverse = jax.scipy.linalg.solve_triangular(lower_factor, identity, lower=True)
    factor = jnp.dot(panel, inverse.T, precision=lax.Precision.HIGHEST, preferred_element_type=panel.dtype)
    row_owner = (jnp.arange(CH_BLOCKS, dtype=jnp.int32) // CBD).astype(jnp.int32)
    half_index = child_map // RBD
    block_index = child_map % RBD
    target = (half_index * (N_ROW * RBD) + row_owner[None, :] * RBD + block_index).astype(jnp.int32)
    blocks = child.reshape(SUBS * CH_BLOCKS, B, WT)
    extend = jax.ops.segment_sum(blocks, target.reshape(-1), num_segments=FB).reshape(NF, WT)
    assembled = trailing + extend
    window = factor[P_SIZE:P_SIZE + WT]
    update = jnp.dot(factor, window.T, precision=lax.Precision.HIGHEST, preferred_element_type=panel.dtype)
    present = pattern.astype(panel.dtype)
    masked = (update.reshape(FB, B, N_COL, B) * present[:, None, :, None]).reshape(NF, WT)
    updated = assembled - masked
    return (factor, updated)
```

```python
import jax
import jax.numpy as jnp
from jax import lax
from jax.experimental import pallas as pl
from jax.experimental.pallas import tpu as pltpu
from jax.sharding import PartitionSpec as P

HI = lax.Precision.HIGHEST
ALL = ("sub", "row", "col")
SB = 128
NX, NY, NZ = 4, 4, 8


def linear(x, core, y, z):
    return (z // 4) * 128 + (x * 2 + core) * 16 + (z % 4) * 4 + y


def pairs_of(move):
    pairs = []
    for x in range(NX):
        for core in range(2):
            for y in range(NY):
                for z in range(NZ):
                    to = move(x, core, y, z)
                    if to is not None:
                        pairs.append((linear(x, core, y, z), linear(*to)))
    return pairs


def send(value, move):
    return lax.ppermute(value, ALL, pairs_of(move))


def contract(a, b, dim_a, dim_b):
    return lax.dot_general(
        a, b, (((dim_a,), (dim_b,)), ((), ())), precision=HI, preferred_element_type=jnp.float32
    )


def block_inverse(strips, group):
    lane = lax.broadcasted_iota(jnp.int32, (8, SB), 1)
    sublane = lax.broadcasted_iota(jnp.int32, (8, SB), 0)
    held = list(strips)
    count = len(held)
    for first in range(0, SB, group):
        own = first // 8
        columns = {}
        for t in range(own, count):
            columns[t] = [
                jnp.broadcast_to(held[t][:, first + m : first + m + 1], (8, SB)) for m in range(group)
            ]
        for m in range(group):
            r = first % 8 + m
            col = first + m
            tops = [jnp.broadcast_to(columns[own][k][r : r + 1, :], (8, SB)) for k in range(m, group)]
            inverse = 1.0 / tops[0]
            row = jnp.broadcast_to(held[own][r : r + 1, :], (8, SB))
            row = jnp.where(lane == col, 1.0, row)
            for t in range(own, count):
                scale = columns[t][m] * inverse
                if t == own:
                    if r == 7:
                        continue
                    scale = jnp.where(sublane > r, scale, 0.0)
                    held[t] = jnp.where((lane == col) & (sublane > r), -scale, held[t] - scale * row)
                else:
                    held[t] = jnp.where(lane == col, 0.0, held[t]) - scale * row
                for k in range(m + 1, group):
                    columns[t][k] = columns[t][k] - scale * tops[k - m]
    out = []
    for t in range(count):
        rows = sublane + 8 * t
        diagonal = jnp.sum(jnp.where(lane == rows, held[t], 0.0), axis=1, keepdims=True)
        unit = jnp.where(lane < rows, held[t], jnp.where(lane == rows, 1.0, 0.0))
        out.append(unit * lax.rsqrt(diagonal))
    return out


def pivot_kernel(parts_ref, inverse_ref, work, lower, diag):
    width = work.shape[0]
    half = width // 2
    left = parts_ref[0]
    right = parts_ref[1]
    work[...] = jnp.zeros_like(work)
    work[0:half, 0:half] = left[:, 0:half]
    work[half : half + SB, 0:half] = left[:, half : half + SB].T
    work[half:, half:] = right[:, 0:half]
    work[half + SB :, 0:SB] = right[0:SB, half:]
    work[half + SB :, SB:half] = right[SB:, half:]
    lower[...] = jnp.zeros_like(lower)
    inverse_ref[...] = jnp.zeros_like(inverse_ref)

    def step(k, carry):
        off = pl.multiple_of(k * SB, SB)
        strips = [work[pl.ds(off + 8 * t, 8), pl.ds(off, SB)] for t in range(SB // 8)]
        done = block_inverse(strips, 8)
        for t in range(SB // 8):
            diag[8 * t : 8 * t + 8, :] = done[t]
        inv = diag[...]
        below = contract(work[:, pl.ds(off, SB)], inv, 1, 1)
        rows = lax.broadcasted_iota(jnp.int32, (width, SB), 0)
        below = jnp.where(rows >= off + SB, below, 0.0)
        lower[:, pl.ds(off, SB)] = below
        work[...] = work[...] - contract(below, below, 1, 1)
        before = contract(lower[pl.ds(off, SB), :], inverse_ref[...], 1, 0)
        inverse_ref[pl.ds(off, SB), :] = -contract(inv, before, 1, 0)
        inverse_ref[pl.ds(off, SB), pl.ds(off, SB)] = inv
        return carry

    lax.fori_loop(0, width // SB, step, 0)


def pivot_inverse(parts):
    width = 2 * parts.shape[1]
    return pl.pallas_call(
        pivot_kernel,
        out_shape=jax.ShapeDtypeStruct((width, width), jnp.float32),
        scratch_shapes=[
            pltpu.VMEM((width, width), jnp.float32),
            pltpu.VMEM((width, width), jnp.float32),
            pltpu.VMEM((SB, SB), jnp.float32),
        ],
        compiler_params=pltpu.CompilerParams(vmem_limit_bytes=32 << 20),
    )(parts)


def solve_kernel(inverse_ref, panel_ref, window_ref, factor_ref, weight_ref):
    inverse = inverse_ref[...]
    factor_ref[...] = contract(panel_ref[...], inverse, 1, 1)
    weight_ref[...] = contract(contract(window_ref[...], inverse, 1, 1), inverse, 1, 0)


def solve(inverse, panel, window):
    shape = jax.ShapeDtypeStruct(panel.shape, jnp.float32)
    return pl.pallas_call(
        solve_kernel,
        out_shape=(shape, jax.ShapeDtypeStruct(window.shape, jnp.float32)),
        compiler_params=pltpu.CompilerParams(vmem_limit_bytes=32 << 20),
    )(inverse, panel, window)


def final_kernel(table, group_ref, weight_ref, trailing_ref, own_ref, other_ref, out_ref):
    i = pl.program_id(0)
    out_ref[...] = trailing_ref[...]

    @pl.when(table[1, i] == 1)
    def _():
        out_ref[...] += own_ref[...]

    @pl.when(table[3, i] == 1)
    def _():
        out_ref[...] += other_ref[...]

    @pl.when(table[5, i] == 1)
    def _():
        out_ref[...] -= contract(group_ref[...], weight_ref[...], 1, 1)


def final(table, group, weight, trailing, own, other):
    size = weight.shape[0]
    width = weight.shape[1]
    blocks = trailing.shape[0] // size
    square = lambda pick: pl.BlockSpec((size, size), pick)
    return pl.pallas_call(
        final_kernel,
        grid_spec=pltpu.PrefetchScalarGridSpec(
            num_scalar_prefetch=1,
            grid=(blocks,),
            in_specs=[
                pl.BlockSpec((size, width), lambda i, t: (t[4, i], 0)),
                pl.BlockSpec((size, width), lambda i, t: (0, 0)),
                square(lambda i, t: (i, 0)),
                square(lambda i, t: (t[0, i], 0)),
                square(lambda i, t: (t[2, i], 0)),
            ],
            out_specs=square(lambda i, t: (i, 0)),
        ),
        out_shape=jax.ShapeDtypeStruct(trailing.shape, jnp.float32),
        compiler_params=pltpu.CompilerParams(vmem_limit_bytes=32 << 20),
    )(table, group, weight, trailing, own, other)


def kept(has, index):
    blocks = has.shape[0]
    coded = jnp.where(has, jnp.arange(blocks, dtype=jnp.int32) * blocks + index, -1)
    place = jnp.arange(blocks)
    latest = jnp.max(jnp.where(place[None, :] <= place[:, None], coded[None, :], -1), axis=1)
    return jnp.where(latest >= 0, latest % blocks, 0)


def lookup(slots, base, blocks):
    match = slots[None, :] == base + jnp.arange(blocks, dtype=jnp.int32)[:, None]
    has = jnp.any(match, axis=1)
    index = jnp.argmax(match, axis=1).astype(jnp.int32)
    return kept(has, index), has.astype(jnp.int32)


def pivot_parts(panel, x, core, y, z):
    half = panel.shape[1] // 2
    packed = jnp.concatenate([panel[SB:, 0:SB], panel[SB:, SB:half]], axis=0)
    from_left = panel[:, : half + SB]
    from_right = jnp.concatenate([panel[:, half:], packed], axis=1)
    whole = jnp.where(y == 0, from_left, from_right)
    split = send(
        whole[SB:], lambda x, c, y, z: (x, 1, y, z) if x == 0 and c == 0 and z == 0 and y < 2 else None
    )
    held = jnp.where(core == 0, whole[:SB], split)

    orders = (
        (("z", 4), ("z", 2), ("z", 1), ("x", 2), ("x", 1), ("y", 2)),
        (("x", 2), ("x", 1), ("y", 2), ("z", 4), ("z", 2), ("z", 1)),
    )
    have = {(0, c, y, 0) for c in range(2) for y in range(2)}
    for number in range(len(orders[0])):
        targets = {}
        for place in sorted(have):
            axis, stride = orders[place[1]][number]
            where = "xcyz".index(axis)
            to = list(place)
            to[where] += stride
            targets[place] = tuple(to)
        got = send(held, lambda x, c, y, z: targets.get((x, c, y, z)))
        receives = False
        for c in range(2):
            axis, stride = orders[c][number]
            coordinate = {"x": x, "y": y, "z": z}[axis]
            receives = receives | ((core == c) & ((coordinate // stride) % 2 == 1))
        held = jnp.where(receives, got, held)
        have = have | set(targets.values())
    other = send(held, lambda x, c, y, z: (x, c, y ^ 1, z))
    left = jnp.where(y % 2 == 0, held, other)
    right = jnp.where(y % 2 == 0, other, held)
    mine = jnp.stack([left, right])
    theirs = send(mine, lambda x, c, y, z: (x, 1 - c, y, z))
    top = jnp.where(core == 0, mine, theirs)
    bottom = jnp.where(core == 0, theirs, mine)
    return jnp.concatenate([top, bottom], axis=1)


def window_rows(panel, x, core, z):
    place = {}
    for col in range(16):
        block = 2 + col
        place[(block // 16) * 16 + block % 16] = col
    held = lax.ppermute(panel, ALL, sorted(place.items()))
    got = send(held, lambda x, c, y, z: (x, c, y, z + 4) if x == 0 and c == 0 and z < 4 else None)
    held = jnp.where(z >= 4, got, held)
    got = send(held, lambda x, c, y, z: (2, c, y, z) if x == 0 and c == 0 else None)
    held = jnp.where(x == 2, got, held)
    got = send(held, lambda x, c, y, z: (x + 1, c, y, z) if x % 2 == 0 and c == 0 else None)
    held = jnp.where(x % 2 == 1, got, held)
    got = send(held, lambda x, c, y, z: (x, 1, y, z) if c == 0 else None)
    return jnp.where(core == 1, got, held)


def local(panel, trailing, child, child_map, pattern):
    size = trailing.shape[1]
    blocks = trailing.shape[0] // size
    sub = lax.axis_index("sub")
    row = lax.axis_index("row")
    col = lax.axis_index("col")
    x, core, y, z = row // 2, row % 2, col % NY, sub * 4 + col // NY
    swap = lambda x, c, y, z: (x, c, y, (z + 4) % NZ)
    parts = pivot_parts(panel, x, core, y, z)
    other_child = send(child[0], swap)
    other_map = send(child_map, swap)
    group = lax.all_gather(panel, "col", axis=0, tiled=True)
    window = window_rows(panel, x, core, z)
    base = sub * blocks
    own_index, own_has = lookup(child_map[0], base, blocks)
    other_index, other_has = lookup(other_map[0], base, blocks)
    present = pattern[:, 0] == 1
    rows_index = kept(present, jnp.arange(blocks, dtype=jnp.int32))
    table = jnp.stack(
        [own_index, own_has, other_index, other_has, rows_index, present.astype(jnp.int32)]
    )
    inverse = pivot_inverse(parts)
    factor, weight = solve(inverse, panel, window)
    updated = final(table, group, weight, trailing, child[0], other_child)
    return (factor, updated)


def solution(mesh):
    return jax.shard_map(
        local,
        mesh=mesh,
        in_specs=(
            P(("sub", "row", "col"), None),
            P(("sub", "row"), "col"),
            P("sub", "row", "col"),
            P("sub", "row"),
            P(("sub", "row"), "col"),
        ),
        out_specs=(P(("sub", "row", "col"), None), P(("sub", "row"), "col")),
        check_vma=False,
    )
```

```python
import jax
import jax.numpy as jnp
from jax import lax
from jax.experimental import pallas as pl
from jax.experimental.pallas import tpu as pltpu
from jax.sharding import PartitionSpec as P

HI = lax.Precision.HIGHEST
ALL = ("sub", "row", "col")
SB = 128
NX, NY, NZ = 4, 4, 8


def linear(x, core, y, z):
    return (z // 4) * 128 + (x * 2 + core) * 16 + (z % 4) * 4 + y


def pairs_of(move):
    pairs = []
    for x in range(NX):
        for core in range(2):
            for y in range(NY):
                for z in range(NZ):
                    to = move(x, core, y, z)
                    if to is not None:
                        pairs.append((linear(x, core, y, z), linear(*to)))
    return pairs


def send(value, move):
    return lax.ppermute(value, ALL, pairs_of(move))


def contract(a, b, dim_a, dim_b):
    return lax.dot_general(
        a, b, (((dim_a,), (dim_b,)), ((), ())), precision=HI, preferred_element_type=jnp.float32
    )


def block_inverse(strips, group):
    lane = lax.broadcasted_iota(jnp.int32, (8, SB), 1)
    sublane = lax.broadcasted_iota(jnp.int32, (8, SB), 0)
    held = list(strips)
    count = len(held)
    for first in range(0, SB, group):
        own = first // 8
        columns = {}
        for t in range(own, count):
            columns[t] = [
                jnp.broadcast_to(held[t][:, first + m : first + m + 1], (8, SB)) for m in range(group)
            ]
        for m in range(group):
            r = first % 8 + m
            col = first + m
            tops = [jnp.broadcast_to(columns[own][k][r : r + 1, :], (8, SB)) for k in range(m, group)]
            inverse = 1.0 / tops[0]
            row = jnp.broadcast_to(held[own][r : r + 1, :], (8, SB))
            row = jnp.where(lane == col, 1.0, row)
            for t in range(own, count):
                scale = columns[t][m] * inverse
                if t == own:
                    if r == 7:
                        continue
                    scale = jnp.where(sublane > r, scale, 0.0)
                    held[t] = jnp.where((lane == col) & (sublane > r), -scale, held[t] - scale * row)
                else:
                    held[t] = jnp.where(lane == col, 0.0, held[t]) - scale * row
                for k in range(m + 1, group):
                    columns[t][k] = columns[t][k] - scale * tops[k - m]
    out = []
    for t in range(count):
        rows = sublane + 8 * t
        diagonal = jnp.sum(jnp.where(lane == rows, held[t], 0.0), axis=1, keepdims=True)
        unit = jnp.where(lane < rows, held[t], jnp.where(lane == rows, 1.0, 0.0))
        out.append(unit * lax.rsqrt(diagonal))
    return out


def pivot_kernel(parts_ref, inverse_ref, work, lower, diag):
    width = work.shape[0]
    half = width // 2
    left = parts_ref[0]
    right = parts_ref[1]
    work[...] = jnp.zeros_like(work)
    work[0:half, 0:half] = left[:, 0:half]
    work[half : half + SB, 0:half] = left[:, half : half + SB].T
    work[half:, half:] = right[:, 0:half]
    work[half + SB :, 0:SB] = right[0:SB, half:]
    work[half + SB :, SB:half] = right[SB:, half:]
    lower[...] = jnp.zeros_like(lower)
    inverse_ref[...] = jnp.zeros_like(inverse_ref)

    def step(k, carry):
        off = pl.multiple_of(k * SB, SB)
        strips = [work[pl.ds(off + 8 * t, 8), pl.ds(off, SB)] for t in range(SB // 8)]
        done = block_inverse(strips, 8)
        for t in range(SB // 8):
            diag[8 * t : 8 * t + 8, :] = done[t]
        inv = diag[...]
        below = contract(work[:, pl.ds(off, SB)], inv, 1, 1)
        rows = lax.broadcasted_iota(jnp.int32, (width, SB), 0)
        below = jnp.where(rows >= off + SB, below, 0.0)
        lower[:, pl.ds(off, SB)] = below
        work[...] = work[...] - contract(below, below, 1, 1)
        before = contract(lower[pl.ds(off, SB), :], inverse_ref[...], 1, 0)
        inverse_ref[pl.ds(off, SB), :] = -contract(inv, before, 1, 0)
        inverse_ref[pl.ds(off, SB), pl.ds(off, SB)] = inv
        return carry

    lax.fori_loop(0, width // SB, step, 0)


def pivot_inverse(parts):
    width = 2 * parts.shape[1]
    return pl.pallas_call(
        pivot_kernel,
        out_shape=jax.ShapeDtypeStruct((width, width), jnp.float32),
        scratch_shapes=[
            pltpu.VMEM((width, width), jnp.float32),
            pltpu.VMEM((width, width), jnp.float32),
            pltpu.VMEM((SB, SB), jnp.float32),
        ],
        compiler_params=pltpu.CompilerParams(vmem_limit_bytes=32 << 20),
    )(parts)


def solve_kernel(inverse_ref, panel_ref, window_ref, factor_ref, weight_ref):
    inverse = inverse_ref[...]
    factor_ref[...] = contract(panel_ref[...], inverse, 1, 1)
    weight_ref[...] = contract(contract(window_ref[...], inverse, 1, 1), inverse, 1, 0)


def solve(inverse, panel, window):
    shape = jax.ShapeDtypeStruct(panel.shape, jnp.float32)
    return pl.pallas_call(
        solve_kernel,
        out_shape=(shape, jax.ShapeDtypeStruct(window.shape, jnp.float32)),
        compiler_params=pltpu.CompilerParams(vmem_limit_bytes=32 << 20),
    )(inverse, panel, window)


def update_kernel(table, zl, near_ref, far_ref, weight_ref, trailing_ref, own_ref, out_ref):
    i = pl.program_id(0)
    is_near = i // NY == zl[0]
    out_ref[...] = trailing_ref[...]

    @pl.when(table[1, i] == 1)
    def _():
        out_ref[...] += own_ref[...]

    @pl.when((table[4, i] == 1) & is_near)
    def _():
        out_ref[...] -= contract(near_ref[...], weight_ref[...], 1, 1)

    @pl.when((table[4, i] == 1) & jnp.logical_not(is_near))
    def _():
        out_ref[...] -= contract(far_ref[...], weight_ref[...], 1, 1)


def near_place(i, table, zl):
    return (jnp.where(i // NY == zl[0], i % NY, 0), 0)


def far_place(i, table, zl):
    shift = (i // NY) ^ zl[0]
    return (jnp.where(shift == 0, 0, (i % NY) * 3 + shift - 1), 0)


def update(table, zl, near, far, weight, trailing, own):
    size = weight.shape[0]
    width = weight.shape[1]
    blocks = trailing.shape[0] // size
    square = lambda pick: pl.BlockSpec((size, size), pick)
    return pl.pallas_call(
        update_kernel,
        grid_spec=pltpu.PrefetchScalarGridSpec(
            num_scalar_prefetch=2,
            grid=(blocks,),
            in_specs=[
                pl.BlockSpec((size, width), near_place),
                pl.BlockSpec((size, width), far_place),
                pl.BlockSpec((size, width), lambda i, t, zl: (0, 0)),
                square(lambda i, t, zl: (i, 0)),
                square(lambda i, t, zl: (t[0, i], 0)),
            ],
            out_specs=square(lambda i, t, zl: (i, 0)),
        ),
        out_shape=jax.ShapeDtypeStruct(trailing.shape, jnp.float32),
        compiler_params=pltpu.CompilerParams(vmem_limit_bytes=56 << 20),
    )(table, zl, near, far, weight, trailing, own)


def extend_kernel(table, assembled_ref, other_ref, out_ref):
    i = pl.program_id(0)
    out_ref[...] = assembled_ref[...]

    @pl.when(table[2, i] == 1)
    def _():
        out_ref[...] += other_ref[...]


def extend(table, assembled, other):
    size = assembled.shape[1]
    square = lambda pick: pl.BlockSpec((size, size), pick)
    return pl.pallas_call(
        extend_kernel,
        grid_spec=pltpu.PrefetchScalarGridSpec(
            num_scalar_prefetch=1,
            grid=(assembled.shape[0] // size,),
            in_specs=[square(lambda i, t: (i, 0)), square(lambda i, t: (t[3, i], 0))],
            out_specs=square(lambda i, t: (i, 0)),
        ),
        out_shape=jax.ShapeDtypeStruct(assembled.shape, jnp.float32),
        input_output_aliases={1: 0},
        compiler_params=pltpu.CompilerParams(vmem_limit_bytes=56 << 20),
    )(table, assembled, other)


def kept(has, index):
    blocks = has.shape[0]
    coded = jnp.where(has, jnp.arange(blocks, dtype=jnp.int32) * blocks + index, -1)
    place = jnp.arange(blocks)
    latest = jnp.max(jnp.where(place[None, :] <= place[:, None], coded[None, :], -1), axis=1)
    return jnp.where(latest >= 0, latest % blocks, 0)


def lookup(slots, base, blocks):
    match = slots[None, :] == base + jnp.arange(blocks, dtype=jnp.int32)[:, None]
    has = jnp.any(match, axis=1)
    index = jnp.argmax(match, axis=1).astype(jnp.int32)
    return kept(has, index), has.astype(jnp.int32)


STEPS = (("z", 4), ("z", 2), ("z", 1), ("y", 2), ("x", 2), ("x", 1))


def pivot_split(panel, core, y):
    half = panel.shape[1] // 2
    packed = jnp.concatenate([panel[SB:, 0:SB], panel[SB:, SB:half]], axis=0)
    from_left = panel[:, : half + SB]
    from_right = jnp.concatenate([panel[:, half:], packed], axis=1)
    whole = jnp.where(y == 0, from_left, from_right)
    split = send(
        whole[SB:], lambda x, c, y, z: (x, 1, y, z) if x == 0 and c == 0 and z == 0 and y < 2 else None
    )
    return jnp.where(core == 0, whole[:SB], split)


def pivot_spread(held, numbers, x, y, z):
    have = {(0, c, y, 0) for c in range(2) for y in range(2)}
    for number, (axis, stride) in enumerate(STEPS):
        targets = {}
        for place in sorted(have):
            to = list(place)
            to["xcyz".index(axis)] += stride
            targets[place] = tuple(to)
        have = have | set(targets.values())
        if number not in numbers:
            continue
        got = send(held, lambda x, c, y, z: targets.get((x, c, y, z)))
        coordinate = {"x": x, "y": y, "z": z}[axis]
        held = jnp.where((coordinate // stride) % 2 == 1, got, held)
    return held


def join_y(held, y):
    other = send(held, lambda x, c, y, z: (x, c, y ^ 1, z) if x == 0 else None)
    left = jnp.where(y % 2 == 0, held, other)
    right = jnp.where(y % 2 == 0, other, held)
    return jnp.stack([left, right])


def join_core(mine, core):
    theirs = send(mine, lambda x, c, y, z: (x, 1 - c, y, z))
    top = jnp.where(core == 0, mine, theirs)
    bottom = jnp.where(core == 0, theirs, mine)
    return jnp.concatenate([top, bottom], axis=1)


def window_halves(panel, z):
    place = {}
    for col in range(16):
        block = 2 + col
        place[(block // 16) * 16 + block % 16] = col
    held = lax.ppermute(panel, ALL, sorted(place.items()))
    got = send(held, lambda x, c, y, z: (x, c, y, z + 4) if x == 0 and c == 0 and z < 4 else None)
    return jnp.where(z >= 4, got, held)


def window_rows(held, x, core):
    got = send(held, lambda x, c, y, z: (2, c, y, z) if x == 0 and c == 0 else None)
    held = jnp.where(x == 2, got, held)
    got = send(held, lambda x, c, y, z: (x + 1, c, y, z) if x % 2 == 0 and c == 0 else None)
    held = jnp.where(x % 2 == 1, got, held)
    got = send(held, lambda x, c, y, z: (x, 1, y, z) if c == 0 else None)
    return jnp.where(core == 1, got, held)


def gather_y(value):
    groups = [[zl * NY + y for y in range(NY)] for zl in range(NZ // 2)]
    return lax.all_gather(value, "col", axis_index_groups=groups, axis=0, tiled=True)


def local(panel, trailing, child, child_map, pattern):
    size = trailing.shape[1]
    blocks = trailing.shape[0] // size
    sub = lax.axis_index("sub")
    row = lax.axis_index("row")
    col = lax.axis_index("col")
    x, core, y, z = row // 2, row % 2, col % NY, sub * 4 + col // NY
    swap = lambda x, c, y, z: (x, c, y, (z + 4) % NZ)
    near = gather_y(panel)
    held = pivot_split(panel, core, y)
    window = window_halves(panel, z)
    other_map = send(child_map, swap)
    held = pivot_spread(held, (0, 1, 2), x, y, z)
    held, window, later = lax.optimization_barrier((held, window, panel))
    across = [send(later, lambda x, c, y, z, d=d: (x, c, y, z ^ d)) for d in (1, 2, 3)]
    held = pivot_spread(held, (3,), x, y, z)
    held, across[0] = lax.optimization_barrier((held, across[0]))
    held = join_y(held, y)
    held, across[1] = lax.optimization_barrier((held, across[1]))
    held = pivot_spread(held, (4,), x, y, z)
    held, across[2] = lax.optimization_barrier((held, across[2]))
    far = gather_y(jnp.concatenate(across, axis=0))
    other_child = send(child[0], swap)
    held = pivot_spread(held, (5,), x, y, z)
    parts = join_core(held, core)
    window = window_rows(window, x, core)
    base = sub * blocks
    own_index, own_has = lookup(child_map[0], base, blocks)
    other_index, other_has = lookup(other_map[0], base, blocks)
    present = pattern[:, 0] == 1
    table = jnp.stack(
        [own_index, own_has, other_has, other_index, present.astype(jnp.int32)]
    )
    inverse = pivot_inverse(parts)
    factor, weight = solve(inverse, panel, window)
    zl = jnp.broadcast_to(z % 4, (1,)).astype(jnp.int32)
    assembled = update(table, zl, near, far, weight, trailing, child[0])
    updated = extend(table, assembled, other_child)
    return (factor, updated)


def solution(mesh):
    return jax.shard_map(
        local,
        mesh=mesh,
        in_specs=(
            P(("sub", "row", "col"), None),
            P(("sub", "row"), "col"),
            P("sub", "row", "col"),
            P("sub", "row"),
            P(("sub", "row"), "col"),
        ),
        out_specs=(P(("sub", "row", "col"), None), P(("sub", "row"), "col")),
        check_vma=False,
    )
```

```python
import jax
import jax.numpy as jnp
from jax import lax
from jax.experimental import pallas as pl
from jax.experimental.pallas import tpu as pltpu
from jax.sharding import PartitionSpec as P

HI = lax.Precision.HIGHEST
ALL = ("sub", "row", "col")
SB = 128
NX, NY, NZ = 4, 4, 8
FIRST, MAIN = 1, 6


def linear(x, core, y, z):
    return (z // 4) * 128 + (x * 2 + core) * 16 + (z % 4) * 4 + y


def pairs_of(move):
    pairs = []
    for x in range(NX):
        for core in range(2):
            for y in range(NY):
                for z in range(NZ):
                    to = move(x, core, y, z)
                    if to is not None:
                        pairs.append((linear(x, core, y, z), linear(*to)))
    return pairs


def send(value, move):
    return lax.ppermute(value, ALL, pairs_of(move))


def contract(a, b, dim_a, dim_b):
    return lax.dot_general(
        a, b, (((dim_a,), (dim_b,)), ((), ())), precision=HI, preferred_element_type=jnp.float32
    )


def block_inverse(strips, group):
    lane = lax.broadcasted_iota(jnp.int32, (8, SB), 1)
    sublane = lax.broadcasted_iota(jnp.int32, (8, SB), 0)
    held = list(strips)
    count = len(held)
    for first in range(0, SB, group):
        own = first // 8
        columns = {}
        for t in range(own, count):
            columns[t] = [
                jnp.broadcast_to(held[t][:, first + m : first + m + 1], (8, SB)) for m in range(group)
            ]
        for m in range(group):
            r = first % 8 + m
            col = first + m
            tops = [jnp.broadcast_to(columns[own][k][r : r + 1, :], (8, SB)) for k in range(m, group)]
            inverse = 1.0 / tops[0]
            row = jnp.broadcast_to(held[own][r : r + 1, :], (8, SB))
            row = jnp.where(lane == col, 1.0, row)
            for t in range(own, count):
                scale = columns[t][m] * inverse
                if t == own:
                    if r == 7:
                        continue
                    scale = jnp.where(sublane > r, scale, 0.0)
                    held[t] = jnp.where((lane == col) & (sublane > r), -scale, held[t] - scale * row)
                else:
                    held[t] = jnp.where(lane == col, 0.0, held[t]) - scale * row
                for k in range(m + 1, group):
                    columns[t][k] = columns[t][k] - scale * tops[k - m]
    out = []
    for t in range(count):
        rows = sublane + 8 * t
        diagonal = jnp.sum(jnp.where(lane == rows, held[t], 0.0), axis=1, keepdims=True)
        unit = jnp.where(lane < rows, held[t], jnp.where(lane == rows, 1.0, 0.0))
        out.append(unit * lax.rsqrt(diagonal))
    return out


def pivot_kernel(parts_ref, inverse_ref, work, lower, diag):
    width = work.shape[0]
    half = width // 2
    left = parts_ref[0]
    right = parts_ref[1]
    work[...] = jnp.zeros_like(work)
    work[0:half, 0:half] = left[:, 0:half]
    work[half : half + SB, 0:half] = left[:, half : half + SB].T
    work[half:, half:] = right[:, 0:half]
    work[half + SB :, 0:SB] = right[0:SB, half:]
    work[half + SB :, SB:half] = right[SB:, half:]
    lower[...] = jnp.zeros_like(lower)
    inverse_ref[...] = jnp.zeros_like(inverse_ref)

    def step(k, carry):
        off = pl.multiple_of(k * SB, SB)
        strips = [work[pl.ds(off + 8 * t, 8), pl.ds(off, SB)] for t in range(SB // 8)]
        done = block_inverse(strips, 8)
        for t in range(SB // 8):
            diag[8 * t : 8 * t + 8, :] = done[t]
        inv = diag[...]
        below = contract(work[:, pl.ds(off, SB)], inv, 1, 1)
        rows = lax.broadcasted_iota(jnp.int32, (width, SB), 0)
        below = jnp.where(rows >= off + SB, below, 0.0)
        lower[:, pl.ds(off, SB)] = below
        work[...] = work[...] - contract(below, below, 1, 1)
        before = contract(lower[pl.ds(off, SB), :], inverse_ref[...], 1, 0)
        inverse_ref[pl.ds(off, SB), :] = -contract(inv, before, 1, 0)
        inverse_ref[pl.ds(off, SB), pl.ds(off, SB)] = inv
        return carry

    lax.fori_loop(0, width // SB, step, 0)


def pivot_inverse(parts):
    width = 2 * parts.shape[1]
    return pl.pallas_call(
        pivot_kernel,
        out_shape=jax.ShapeDtypeStruct((width, width), jnp.float32),
        scratch_shapes=[
            pltpu.VMEM((width, width), jnp.float32),
            pltpu.VMEM((width, width), jnp.float32),
            pltpu.VMEM((SB, SB), jnp.float32),
        ],
        compiler_params=pltpu.CompilerParams(vmem_limit_bytes=32 << 20),
    )(parts)


def solve_kernel(inverse_ref, panel_ref, window_ref, factor_ref, weight_ref):
    inverse = inverse_ref[...]
    factor_ref[...] = contract(panel_ref[...], inverse, 1, 1)
    weight_ref[...] = contract(contract(window_ref[...], inverse, 1, 1), inverse, 1, 0)


def solve(inverse, panel, window):
    shape = jax.ShapeDtypeStruct(panel.shape, jnp.float32)
    return pl.pallas_call(
        solve_kernel,
        out_shape=(shape, jax.ShapeDtypeStruct(window.shape, jnp.float32)),
        compiler_params=pltpu.CompilerParams(vmem_limit_bytes=32 << 20),
    )(inverse, panel, window)


def take_kernel(order, block_ref, out_ref):
    out_ref[...] = block_ref[...]


def take_blocks(order, blocks, size):
    count = order.shape[0]
    return pl.pallas_call(
        take_kernel,
        grid_spec=pltpu.PrefetchScalarGridSpec(
            num_scalar_prefetch=1,
            grid=(count,),
            in_specs=[pl.BlockSpec((size, size), lambda i, t: (t[i], 0))],
            out_specs=pl.BlockSpec((size, size), lambda i, t: (i, 0)),
        ),
        out_shape=jax.ShapeDtypeStruct((count * size, size), jnp.float32),
        compiler_params=pltpu.CompilerParams(vmem_limit_bytes=56 << 20),
    )(order, blocks)


BLOCK, OWN, OWN_HAS, FROM, FROM_HAS, PRESENT, ROWS = 0, 1, 2, (3, 4, 5), 6, 7, 8
NEAR = 8


def near_kernel(table, rows_ref, weight_ref, trailing_ref, own_ref, out_ref):
    i = pl.program_id(0)
    out_ref[...] = trailing_ref[...]

    @pl.when(table[OWN_HAS, i] == 1)
    def _():
        out_ref[...] += own_ref[...]

    @pl.when(table[PRESENT, i] == 1)
    def _():
        out_ref[...] -= contract(rows_ref[...], weight_ref[...], 1, 1)


def update_near(table, near, weight, trailing, own):
    size, width = weight.shape
    square = lambda pick: pl.BlockSpec((size, size), pick)
    return pl.pallas_call(
        near_kernel,
        grid_spec=pltpu.PrefetchScalarGridSpec(
            num_scalar_prefetch=1,
            grid=(NEAR,),
            in_specs=[
                pl.BlockSpec((size, width), lambda i, t: (t[ROWS, i], 0)),
                pl.BlockSpec((size, width), lambda i, t: (0, 0)),
                square(lambda i, t: (t[BLOCK, i], 0)),
                square(lambda i, t: (t[OWN, i], 0)),
            ],
            out_specs=square(lambda i, t: (t[BLOCK, i], 0)),
        ),
        out_shape=jax.ShapeDtypeStruct(trailing.shape, jnp.float32),
        compiler_params=pltpu.CompilerParams(vmem_limit_bytes=56 << 20),
    )(table, near, weight, trailing, own)


def far_kernel(table, done_ref, rows_ref, weight_ref, trailing_ref, own_ref, first_ref, main_ref, rest_ref, out_ref):
    i = pl.program_id(0)

    @pl.when(i < NEAR)
    def _():
        out_ref[...] = done_ref[...]

    @pl.when(i >= NEAR)
    def _():
        out_ref[...] = trailing_ref[...]

        @pl.when(table[OWN_HAS, i] == 1)
        def _():
            out_ref[...] += own_ref[...]

        @pl.when(table[PRESENT, i] == 1)
        def _():
            out_ref[...] -= contract(rows_ref[...], weight_ref[...], 1, 1)

    for number, other_ref in enumerate((first_ref, main_ref, rest_ref)):

        @pl.when(table[FROM_HAS, i] == number + 1)
        def _():
            out_ref[...] += other_ref[...]


def update_far(table, done, far, weight, trailing, own, others):
    size, width = weight.shape
    last = NEAR - 1
    square = lambda pick: pl.BlockSpec((size, size), pick)
    return pl.pallas_call(
        far_kernel,
        grid_spec=pltpu.PrefetchScalarGridSpec(
            num_scalar_prefetch=1,
            grid=(trailing.shape[0] // size,),
            in_specs=[
                square(lambda i, t: (t[BLOCK, jnp.minimum(i, last)], 0)),
                pl.BlockSpec((size, width), lambda i, t: (t[ROWS, jnp.maximum(i, NEAR)], 0)),
                pl.BlockSpec((size, width), lambda i, t: (0, 0)),
                square(lambda i, t: (t[BLOCK, jnp.maximum(i, NEAR)], 0)),
                square(lambda i, t: (t[OWN, jnp.maximum(i, NEAR)], 0)),
                *[square(lambda i, t, at=at: (t[at, i], 0)) for at in FROM],
            ],
            out_specs=square(lambda i, t: (t[BLOCK, i], 0)),
        ),
        out_shape=jax.ShapeDtypeStruct(trailing.shape, jnp.float32),
        input_output_aliases={1: 0},
        compiler_params=pltpu.CompilerParams(vmem_limit_bytes=56 << 20),
    )(table, done, far, weight, trailing, own, *others)


def kept(has, index):
    blocks = has.shape[0]
    coded = jnp.where(has, jnp.arange(blocks, dtype=jnp.int32) * blocks + index, -1)
    place = jnp.arange(blocks)
    latest = jnp.max(jnp.where(place[None, :] <= place[:, None], coded[None, :], -1), axis=1)
    return jnp.where(latest >= 0, latest % blocks, 0)


def lookup(slots, target):
    match = slots[None, :] == target[:, None]
    return jnp.any(match, axis=1), jnp.argmax(match, axis=1).astype(jnp.int32)


def crossing(slots, home, blocks):
    cross = slots // blocks != home
    k = jnp.arange(slots.shape[0])
    earlier = k[None, :] < k[:, None]
    ahead = jnp.sum(earlier & cross[None, :], axis=1)
    count = jnp.sum(cross)
    place = jnp.where(cross, ahead, count + k - ahead)
    order = jnp.sum(jnp.where(place[None, :] == k[:, None], k[None, :], 0), axis=1)
    return count, place.astype(jnp.int32), order.astype(jnp.int32)


STEPS = (("z", 4), ("z", 2), ("z", 1), ("y", 2), ("x", 2), ("x", 1))


def pivot_split(panel, core, y):
    half = panel.shape[1] // 2
    packed = jnp.concatenate([panel[SB:, 0:SB], panel[SB:, SB:half]], axis=0)
    from_left = panel[:, : half + SB]
    from_right = jnp.concatenate([panel[:, half:], packed], axis=1)
    whole = jnp.where(y == 0, from_left, from_right)
    split = send(
        whole[SB:], lambda x, c, y, z: (x, 1, y, z) if x == 0 and c == 0 and z == 0 and y < 2 else None
    )
    return jnp.where(core == 0, whole[:SB], split)


def pivot_spread(held, numbers, x, y, z):
    have = {(0, c, y, 0) for c in range(2) for y in range(2)}
    for number, (axis, stride) in enumerate(STEPS):
        targets = {}
        for place in sorted(have):
            to = list(place)
            to["xcyz".index(axis)] += stride
            targets[place] = tuple(to)
        have = have | set(targets.values())
        if number not in numbers:
            continue
        got = send(held, lambda x, c, y, z: targets.get((x, c, y, z)))
        coordinate = {"x": x, "y": y, "z": z}[axis]
        held = jnp.where((coordinate // stride) % 2 == 1, got, held)
    return held


def join_y(held, y):
    other = send(held, lambda x, c, y, z: (x, c, y ^ 1, z) if x == 0 else None)
    left = jnp.where(y % 2 == 0, held, other)
    right = jnp.where(y % 2 == 0, other, held)
    return jnp.stack([left, right])


def join_core(mine, core):
    theirs = send(mine, lambda x, c, y, z: (x, 1 - c, y, z))
    top = jnp.where(core == 0, mine, theirs)
    bottom = jnp.where(core == 0, theirs, mine)
    return jnp.concatenate([top, bottom], axis=1)


def window_owned(panel):
    place = {}
    for col in range(16):
        block = 2 + col
        place[(block // 16) * 16 + block % 16] = col
    return lax.ppermute(panel, ALL, sorted(place.items()))


def window_halves(held, z):
    got = send(held, lambda x, c, y, z: (x, c, y, z + 4) if x == 0 and c == 0 and z < 4 else None)
    return jnp.where(z >= 4, got, held)


def window_rows(held, x, core):
    got = send(held, lambda x, c, y, z: (2, c, y, z) if x == 0 and c == 0 else None)
    held = jnp.where(x == 2, got, held)
    got = send(held, lambda x, c, y, z: (x + 1, c, y, z) if x % 2 == 0 and c == 0 else None)
    held = jnp.where(x % 2 == 1, got, held)
    got = send(held, lambda x, c, y, z: (x, 1, y, z) if c == 0 else None)
    return jnp.where(core == 1, got, held)


def gather_y(value):
    groups = [[zl * NY + y for y in range(NY)] for zl in range(NZ // 2)]
    return lax.all_gather(value, "col", axis_index_groups=groups, axis=0, tiled=True)


def swap(value):
    return send(value, lambda x, c, y, z: (x, c, y, (z + 4) % NZ))


def send_rest(order, child, size, both):
    first = swap(take_blocks(order[:1], child, size))
    second = lax.cond(
        both, lambda: swap(take_blocks(order[1:], child, size)), lambda: jnp.zeros_like(first)
    )
    return jnp.concatenate([first, second], axis=0)


def local(panel, trailing, child, child_map, pattern):
    size = trailing.shape[1]
    blocks = trailing.shape[0] // size
    sub = lax.axis_index("sub")
    row = lax.axis_index("row")
    col = lax.axis_index("col")
    x, core, y, z = row // 2, row % 2, col % NY, sub * 4 + col // NY
    own_slots = child_map[0]
    own_count, own_place, order = crossing(own_slots, sub, blocks)
    outgoing = take_blocks(order[:MAIN], child[0], size)
    other_slots = swap(child_map)[0]

    tie = lax.optimization_barrier
    exchange = lambda value, d: send(value, lambda x, c, y, z: (x, c, y, z ^ d))
    held = pivot_split(panel, core, y)
    window = window_owned(panel)
    across1 = exchange(panel, 1)
    held = pivot_spread(held, (0,), x, y, z)
    held, window = tie((held, window))
    window = window_halves(window, z)
    held = pivot_spread(held, (1,), x, y, z)
    held, across1, panel2 = tie((held, across1, panel))
    across2 = exchange(panel2, 2)
    near = gather_y(jnp.concatenate([panel, across1], axis=0))
    held = pivot_spread(held, (2,), x, y, z)
    held, across2, window, panel3 = tie((held, across2, window, panel))
    across3 = exchange(panel3, 3)
    held = pivot_spread(held, (3,), x, y, z)
    held, outgoing = tie((held, outgoing))
    first = swap(outgoing[: FIRST * size])
    held = join_y(held, y)
    held, across3 = tie((held, across3))
    far = gather_y(jnp.concatenate([across2, across3], axis=0))
    held = pivot_spread(held, (4,), x, y, z)
    held, first = tie((held, first))
    main = swap(outgoing[FIRST * size :])
    held = pivot_spread(held, (5,), x, y, z)
    parts = join_core(held, core)
    window = window_rows(window, x, core)

    other_count, other_place, _ = crossing(other_slots, 1 - sub, blocks)
    need = jnp.maximum(own_count, other_count)
    step = jnp.arange(blocks, dtype=jnp.int32)
    shift = (step // NEAR) * 2 + step % 2
    block = ((col // NY) ^ shift) * NY + (step % NEAR) // 2
    target = sub * blocks + block
    own_has, own_index = lookup(own_slots, target)
    other_has, other_index = lookup(other_slots, target)
    place = jnp.sum(
        jnp.where(other_index[:, None] == jnp.arange(other_place.shape[0])[None, :], other_place[None, :], 0),
        axis=1,
    )
    starts = (0, FIRST, MAIN)
    ends = (FIRST, MAIN, other_place.shape[0])
    inside = [other_has & (place >= low) & (place < high) for low, high in zip(starts, ends)]
    present = jnp.sum(jnp.where(block[:, None] == step[None, :], pattern[:, 0][None, :], 0), axis=1) == 1
    rows = step % NEAR
    rows = jnp.concatenate([kept(present[:NEAR], rows[:NEAR]), kept(present[NEAR:], rows[NEAR:])])
    table = jnp.stack(
        [
            block,
            kept(own_has, own_index),
            own_has.astype(jnp.int32),
            *[kept(has, place - low) for has, low in zip(inside, starts)],
            sum((number + 1) * has.astype(jnp.int32) for number, has in enumerate(inside)),
            present.astype(jnp.int32),
            rows,
        ]
    ).astype(jnp.int32)

    inverse = pivot_inverse(parts)
    factor, weight = solve(inverse, panel, window)
    done = update_near(table, near, weight, trailing, child[0])
    done, main, need = tie((done, main, need))
    rest = lax.cond(
        need > MAIN,
        lambda: send_rest(order[MAIN:], child[0], size, need > MAIN + 1),
        lambda: jnp.zeros((2 * size, size), jnp.float32),
    )
    updated = update_far(table, done, far, weight, trailing, child[0], (first, main, rest))
    return (factor, updated)


def solution(mesh):
    return jax.shard_map(
        local,
        mesh=mesh,
        in_specs=(
            P(("sub", "row", "col"), None),
            P(("sub", "row"), "col"),
            P("sub", "row", "col"),
            P("sub", "row"),
            P(("sub", "row"), "col"),
        ),
        out_specs=(P(("sub", "row", "col"), None), P(("sub", "row"), "col")),
        check_vma=False,
    )
```

```python
import jax
import jax.numpy as jnp
from jax import lax
from jax.experimental import pallas as pl
from jax.experimental.pallas import tpu as pltpu
from jax.sharding import PartitionSpec as P

HI = lax.Precision.HIGHEST
ALL = ("sub", "row", "col")
SB = 128
NX, NY, NZ = 4, 4, 8
FIRST, MAIN = 2, 6


def linear(x, core, y, z):
    return (z // 4) * 128 + (x * 2 + core) * 16 + (z % 4) * 4 + y


def pairs_of(move):
    pairs = []
    for x in range(NX):
        for core in range(2):
            for y in range(NY):
                for z in range(NZ):
                    to = move(x, core, y, z)
                    if to is not None:
                        pairs.append((linear(x, core, y, z), linear(*to)))
    return pairs


def send(value, move):
    return lax.ppermute(value, ALL, pairs_of(move))


def contract(a, b, dim_a, dim_b):
    return lax.dot_general(
        a, b, (((dim_a,), (dim_b,)), ((), ())), precision=HI, preferred_element_type=jnp.float32
    )


def block_inverse(strips, group):
    lane = lax.broadcasted_iota(jnp.int32, (8, SB), 1)
    sublane = lax.broadcasted_iota(jnp.int32, (8, SB), 0)
    held = list(strips)
    count = len(held)
    for first in range(0, SB, group):
        own = first // 8
        columns = {}
        for t in range(own, count):
            columns[t] = [
                jnp.broadcast_to(held[t][:, first + m : first + m + 1], (8, SB)) for m in range(group)
            ]
        for m in range(group):
            r = first % 8 + m
            col = first + m
            tops = [jnp.broadcast_to(columns[own][k][r : r + 1, :], (8, SB)) for k in range(m, group)]
            inverse = 1.0 / tops[0]
            row = jnp.broadcast_to(held[own][r : r + 1, :], (8, SB))
            row = jnp.where(lane == col, 1.0, row)
            for t in range(own, count):
                scale = columns[t][m] * inverse
                if t == own:
                    if r == 7:
                        continue
                    scale = jnp.where(sublane > r, scale, 0.0)
                    held[t] = jnp.where((lane == col) & (sublane > r), -scale, held[t] - scale * row)
                else:
                    held[t] = jnp.where(lane == col, 0.0, held[t]) - scale * row
                for k in range(m + 1, group):
                    columns[t][k] = columns[t][k] - scale * tops[k - m]
    out = []
    for t in range(count):
        rows = sublane + 8 * t
        diagonal = jnp.sum(jnp.where(lane == rows, held[t], 0.0), axis=1, keepdims=True)
        unit = jnp.where(lane < rows, held[t], jnp.where(lane == rows, 1.0, 0.0))
        out.append(unit * lax.rsqrt(diagonal))
    return out


def pivot_kernel(parts_ref, inverse_ref, work, lower, diag):
    width = work.shape[0]
    half = width // 2
    left = parts_ref[0]
    right = parts_ref[1]
    work[...] = jnp.zeros_like(work)
    work[0:half, 0:half] = left[:, 0:half]
    work[half : half + SB, 0:half] = left[:, half : half + SB].T
    work[half:, half:] = right[:, 0:half]
    work[half + SB :, 0:SB] = right[0:SB, half:]
    work[half + SB :, SB:half] = right[SB:, half:]
    lower[...] = jnp.zeros_like(lower)
    inverse_ref[...] = jnp.zeros_like(inverse_ref)

    def step(k, carry):
        off = pl.multiple_of(k * SB, SB)
        strips = [work[pl.ds(off + 8 * t, 8), pl.ds(off, SB)] for t in range(SB // 8)]
        done = block_inverse(strips, 8)
        for t in range(SB // 8):
            diag[8 * t : 8 * t + 8, :] = done[t]
        inv = diag[...]
        below = contract(work[:, pl.ds(off, SB)], inv, 1, 1)
        rows = lax.broadcasted_iota(jnp.int32, (width, SB), 0)
        below = jnp.where(rows >= off + SB, below, 0.0)
        lower[:, pl.ds(off, SB)] = below
        work[...] = work[...] - contract(below, below, 1, 1)
        before = contract(lower[pl.ds(off, SB), :], inverse_ref[...], 1, 0)
        inverse_ref[pl.ds(off, SB), :] = -contract(inv, before, 1, 0)
        inverse_ref[pl.ds(off, SB), pl.ds(off, SB)] = inv
        return carry

    lax.fori_loop(0, width // SB, step, 0)


def pivot_inverse(parts):
    width = 2 * parts.shape[1]
    return pl.pallas_call(
        pivot_kernel,
        out_shape=jax.ShapeDtypeStruct((width, width), jnp.float32),
        scratch_shapes=[
            pltpu.VMEM((width, width), jnp.float32),
            pltpu.VMEM((width, width), jnp.float32),
            pltpu.VMEM((SB, SB), jnp.float32),
        ],
        compiler_params=pltpu.CompilerParams(vmem_limit_bytes=32 << 20),
    )(parts)


def solve_kernel(inverse_ref, panel_ref, window_ref, factor_ref, weight_ref):
    inverse = inverse_ref[...]
    factor_ref[...] = contract(panel_ref[...], inverse, 1, 1)
    weight_ref[...] = contract(contract(window_ref[...], inverse, 1, 1), inverse, 1, 0)


def solve(inverse, panel, window):
    shape = jax.ShapeDtypeStruct(panel.shape, jnp.float32)
    return pl.pallas_call(
        solve_kernel,
        out_shape=(shape, jax.ShapeDtypeStruct(window.shape, jnp.float32)),
        compiler_params=pltpu.CompilerParams(vmem_limit_bytes=32 << 20),
    )(inverse, panel, window)


def take_kernel(order, block_ref, out_ref):
    out_ref[...] = block_ref[...]


def take_blocks(order, blocks, size):
    count = order.shape[0]
    return pl.pallas_call(
        take_kernel,
        grid_spec=pltpu.PrefetchScalarGridSpec(
            num_scalar_prefetch=1,
            grid=(count,),
            in_specs=[pl.BlockSpec((size, size), lambda i, t: (t[i], 0))],
            out_specs=pl.BlockSpec((size, size), lambda i, t: (i, 0)),
        ),
        out_shape=jax.ShapeDtypeStruct((count * size, size), jnp.float32),
        compiler_params=pltpu.CompilerParams(vmem_limit_bytes=56 << 20),
    )(order, blocks)


BLOCK, OWN, OWN_HAS, FROM, FROM_HAS, PRESENT, ROWS = 0, 1, 2, (3, 4, 5), 6, 7, 8
NEAR = 4


def near_kernel(table, rows_ref, weight_ref, trailing_ref, own_ref, out_ref):
    i = pl.program_id(0)
    out_ref[...] = trailing_ref[...]

    @pl.when(table[OWN_HAS, i] == 1)
    def _():
        out_ref[...] += own_ref[...]

    @pl.when(table[PRESENT, i] == 1)
    def _():
        out_ref[...] -= contract(rows_ref[...], weight_ref[...], 1, 1)


def update_near(table, near, weight, trailing, own):
    size, width = weight.shape
    square = lambda pick: pl.BlockSpec((size, size), pick)
    return pl.pallas_call(
        near_kernel,
        grid_spec=pltpu.PrefetchScalarGridSpec(
            num_scalar_prefetch=1,
            grid=(NEAR,),
            in_specs=[
                pl.BlockSpec((size, width), lambda i, t: (t[ROWS, i], 0)),
                pl.BlockSpec((size, width), lambda i, t: (0, 0)),
                square(lambda i, t: (t[BLOCK, i], 0)),
                square(lambda i, t: (t[OWN, i], 0)),
            ],
            out_specs=square(lambda i, t: (t[BLOCK, i], 0)),
        ),
        out_shape=jax.ShapeDtypeStruct(trailing.shape, jnp.float32),
        compiler_params=pltpu.CompilerParams(vmem_limit_bytes=56 << 20),
    )(table, near, weight, trailing, own)


def far_kernel(table, done_ref, rows_ref, weight_ref, trailing_ref, own_ref, first_ref, main_ref, rest_ref, out_ref):
    i = pl.program_id(0)

    @pl.when(i < NEAR)
    def _():
        out_ref[...] = done_ref[...]

    @pl.when(i >= NEAR)
    def _():
        out_ref[...] = trailing_ref[...]

        @pl.when(table[OWN_HAS, i] == 1)
        def _():
            out_ref[...] += own_ref[...]

        @pl.when(table[PRESENT, i] == 1)
        def _():
            out_ref[...] -= contract(rows_ref[...], weight_ref[...], 1, 1)

    for number, other_ref in enumerate((first_ref, main_ref, rest_ref)):

        @pl.when(table[FROM_HAS, i] == number + 1)
        def _():
            out_ref[...] += other_ref[...]


def update_far(table, done, far, weight, trailing, own, others):
    size, width = weight.shape
    last = NEAR - 1
    square = lambda pick: pl.BlockSpec((size, size), pick)
    return pl.pallas_call(
        far_kernel,
        grid_spec=pltpu.PrefetchScalarGridSpec(
            num_scalar_prefetch=1,
            grid=(trailing.shape[0] // size,),
            in_specs=[
                square(lambda i, t: (t[BLOCK, jnp.minimum(i, last)], 0)),
                pl.BlockSpec((size, width), lambda i, t: (t[ROWS, jnp.maximum(i, NEAR)], 0)),
                pl.BlockSpec((size, width), lambda i, t: (0, 0)),
                square(lambda i, t: (t[BLOCK, jnp.maximum(i, NEAR)], 0)),
                square(lambda i, t: (t[OWN, jnp.maximum(i, NEAR)], 0)),
                *[square(lambda i, t, at=at: (t[at, i], 0)) for at in FROM],
            ],
            out_specs=square(lambda i, t: (t[BLOCK, i], 0)),
        ),
        out_shape=jax.ShapeDtypeStruct(trailing.shape, jnp.float32),
        input_output_aliases={1: 0},
        compiler_params=pltpu.CompilerParams(vmem_limit_bytes=56 << 20),
    )(table, done, far, weight, trailing, own, *others)


def kept(has, index):
    blocks = has.shape[0]
    coded = jnp.where(has, jnp.arange(blocks, dtype=jnp.int32) * blocks + index, -1)
    place = jnp.arange(blocks)
    latest = jnp.max(jnp.where(place[None, :] <= place[:, None], coded[None, :], -1), axis=1)
    return jnp.where(latest >= 0, latest % blocks, 0)


def lookup(slots, target):
    match = slots[None, :] == target[:, None]
    return jnp.any(match, axis=1), jnp.argmax(match, axis=1).astype(jnp.int32)


def crossing(slots, home, blocks):
    cross = slots // blocks != home
    k = jnp.arange(slots.shape[0])
    earlier = k[None, :] < k[:, None]
    ahead = jnp.sum(earlier & cross[None, :], axis=1)
    count = jnp.sum(cross)
    place = jnp.where(cross, ahead, count + k - ahead)
    order = jnp.sum(jnp.where(place[None, :] == k[:, None], k[None, :], 0), axis=1)
    return count, place.astype(jnp.int32), order.astype(jnp.int32)


STEPS = (("z", 4), ("z", 2), ("z", 1), ("y", 2), ("x", 2), ("x", 1))


def pivot_split(panel, core, y):
    half = panel.shape[1] // 2
    packed = jnp.concatenate([panel[SB:, 0:SB], panel[SB:, SB:half]], axis=0)
    from_left = panel[:, : half + SB]
    from_right = jnp.concatenate([panel[:, half:], packed], axis=1)
    whole = jnp.where(y == 0, from_left, from_right)
    split = send(
        whole[SB:], lambda x, c, y, z: (x, 1, y, z) if x == 0 and c == 0 and z == 0 and y < 2 else None
    )
    return jnp.where(core == 0, whole[:SB], split)


def pivot_spread(held, numbers, x, y, z):
    have = {(0, c, y, 0) for c in range(2) for y in range(2)}
    for number, (axis, stride) in enumerate(STEPS):
        targets = {}
        for place in sorted(have):
            to = list(place)
            to["xcyz".index(axis)] += stride
            targets[place] = tuple(to)
        have = have | set(targets.values())
        if number not in numbers:
            continue
        got = send(held, lambda x, c, y, z: targets.get((x, c, y, z)))
        coordinate = {"x": x, "y": y, "z": z}[axis]
        held = jnp.where((coordinate // stride) % 2 == 1, got, held)
    return held


def join_y(held, y):
    other = send(held, lambda x, c, y, z: (x, c, y ^ 1, z) if x == 0 else None)
    left = jnp.where(y % 2 == 0, held, other)
    right = jnp.where(y % 2 == 0, other, held)
    return jnp.stack([left, right])


def join_core(mine, core):
    theirs = send(mine, lambda x, c, y, z: (x, 1 - c, y, z))
    top = jnp.where(core == 0, mine, theirs)
    bottom = jnp.where(core == 0, theirs, mine)
    return jnp.concatenate([top, bottom], axis=1)


def window_owned(panel):
    place = {}
    for col in range(16):
        block = 2 + col
        place[(block // 16) * 16 + block % 16] = col
    return lax.ppermute(panel, ALL, sorted(place.items()))


def window_halves(held, z):
    got = send(held, lambda x, c, y, z: (x, c, y, z + 4) if x == 0 and c == 0 and z < 4 else None)
    return jnp.where(z >= 4, got, held)


def window_x(held, x, stride):
    got = send(
        held, lambda x, c, y, z: (x + stride, c, y, z) if x % (2 * stride) == 0 and c == 0 else None
    )
    return jnp.where((x // stride) % 2 == 1, got, held)


def window_core(held, core):
    got = send(held, lambda x, c, y, z: (x, 1, y, z) if c == 0 else None)
    return jnp.where(core == 1, got, held)


def gather_y(value):
    groups = [[zl * NY + y for y in range(NY)] for zl in range(NZ // 2)]
    return lax.all_gather(value, "col", axis_index_groups=groups, axis=0, tiled=True)


def swap(value):
    return send(value, lambda x, c, y, z: (x, c, y, (z + 4) % NZ))


def send_rest(order, child, size, both):
    first = swap(take_blocks(order[:1], child, size))
    second = lax.cond(
        both, lambda: swap(take_blocks(order[1:], child, size)), lambda: jnp.zeros_like(first)
    )
    return jnp.concatenate([first, second], axis=0)


def local(panel, trailing, child, child_map, pattern):
    size = trailing.shape[1]
    blocks = trailing.shape[0] // size
    sub = lax.axis_index("sub")
    row = lax.axis_index("row")
    col = lax.axis_index("col")
    x, core, y, z = row // 2, row % 2, col % NY, sub * 4 + col // NY
    own_slots = child_map[0]
    own_count, own_place, order = crossing(own_slots, sub, blocks)
    outgoing = take_blocks(order[:MAIN], child[0], size)
    other_slots = swap(child_map)[0]

    tie = lax.optimization_barrier
    zl = z % 4
    right = lambda value, at: send(value, lambda x, c, y, z: (x, c, y, z + 1) if z % 4 in at else None)
    left = lambda value, at: send(value, lambda x, c, y, z: (x, c, y, z - 1) if z % 4 in at else None)
    near = gather_y(panel)
    held = pivot_split(panel, core, y)
    window = window_owned(panel)
    held = pivot_spread(held, (0,), x, y, z)
    held, window = tie((held, window))
    window = window_halves(window, z)
    held = pivot_spread(held, (1, 2), x, y, z)
    held, window, bulk = tie((held, window, panel))
    window = window_x(window, x, 2)
    from_left1, from_right1 = right(bulk, (0, 1, 2)), left(bulk, (1, 2, 3))
    held = pivot_spread(held, (3,), x, y, z)
    held = join_y(held, y)
    held, from_left1, from_right1, near, window = tie((held, from_left1, from_right1, near, window))
    slot1 = jnp.where(zl == 3, from_left1, from_right1)
    window = window_x(window, x, 1)
    from_left2, from_right2 = right(from_left1, (1, 2)), left(from_right1, (1, 2))
    held = pivot_spread(held, (4,), x, y, z)
    held, from_left2, from_right2, window = tie((held, from_left2, from_right2, window))
    window = window_core(window, core)
    ends = send(
        jnp.where(zl == 2, from_left2, from_right2),
        lambda x, c, y, z: {1: (x, c, y, z - 1), 2: (x, c, y, z + 1)}.get(z % 4),
    )
    held = pivot_spread(held, (5,), x, y, z)
    held, ends, outgoing = tie((held, ends, outgoing))
    slot2 = jnp.where(zl == 0, from_right2, jnp.where(zl == 3, from_left2, from_left1))
    slot3 = jnp.where(zl == 1, from_right2, jnp.where(zl == 2, from_left2, ends))
    far = gather_y(jnp.concatenate([slot1, slot2, slot3], axis=0))
    first = swap(outgoing[: FIRST * size])
    parts = join_core(held, core)
    main = swap(outgoing[FIRST * size :])

    other_count, other_place, _ = crossing(other_slots, 1 - sub, blocks)
    need = jnp.maximum(own_count, other_count)
    step = jnp.arange(blocks, dtype=jnp.int32)
    later = jnp.maximum(step - NEAR, 0)
    shift = jnp.where(step < NEAR, 0, 1 + later % 3)
    slots_z = jnp.array([[0, 1, 2, 3], [1, 2, 0, 3], [2, 3, 1, 0], [3, 2, 1, 0]], jnp.int32)[zl]
    step_z = jnp.sum(jnp.where(shift[:, None] == jnp.arange(4)[None, :], slots_z[None, :], 0), axis=1)
    block = step_z * NY + jnp.where(step < NEAR, step, later // 3)
    target = sub * blocks + block
    own_has, own_index = lookup(own_slots, target)
    other_has, other_index = lookup(other_slots, target)
    place = jnp.sum(
        jnp.where(other_index[:, None] == jnp.arange(other_place.shape[0])[None, :], other_place[None, :], 0),
        axis=1,
    )
    starts = (0, FIRST, MAIN)
    ends = (FIRST, MAIN, other_place.shape[0])
    inside = [other_has & (place >= low) & (place < high) for low, high in zip(starts, ends)]
    present = jnp.sum(jnp.where(block[:, None] == step[None, :], pattern[:, 0][None, :], 0), axis=1) == 1
    rows = jnp.concatenate([kept(present[:NEAR], step[:NEAR]), kept(present[NEAR:], later[NEAR:])])
    table = jnp.stack(
        [
            block,
            kept(own_has, own_index),
            own_has.astype(jnp.int32),
            *[kept(has, place - low) for has, low in zip(inside, starts)],
            sum((number + 1) * has.astype(jnp.int32) for number, has in enumerate(inside)),
            present.astype(jnp.int32),
            rows,
        ]
    ).astype(jnp.int32)

    inverse = pivot_inverse(parts)
    factor, weight = solve(inverse, panel, window)
    done = update_near(table, near, weight, trailing, child[0])
    done, main, need = tie((done, main, need))
    rest = lax.cond(
        need > MAIN,
        lambda: send_rest(order[MAIN:], child[0], size, need > MAIN + 1),
        lambda: jnp.zeros((2 * size, size), jnp.float32),
    )
    updated = update_far(table, done, far, weight, trailing, child[0], (first, main, rest))
    return (factor, updated)


def solution(mesh):
    return jax.shard_map(
        local,
        mesh=mesh,
        in_specs=(
            P(("sub", "row", "col"), None),
            P(("sub", "row"), "col"),
            P("sub", "row", "col"),
            P("sub", "row"),
            P(("sub", "row"), "col"),
        ),
        out_specs=(P(("sub", "row", "col"), None), P(("sub", "row"), "col")),
        check_vma=False,
    )
```

```python
import jax
import jax.numpy as jnp
from jax import lax
from jax.experimental import pallas as pl
from jax.experimental.pallas import tpu as pltpu
from jax.sharding import PartitionSpec as P

HI = lax.Precision.HIGHEST
ALL = ("sub", "row", "col")
SB = 128
NX, NY, NZ = 4, 4, 8
FIRST, MAIN = 1, 6


def linear(x, core, y, z):
    return (z // 4) * 128 + (x * 2 + core) * 16 + (z % 4) * 4 + y


def pairs_of(move):
    pairs = []
    for x in range(NX):
        for core in range(2):
            for y in range(NY):
                for z in range(NZ):
                    to = move(x, core, y, z)
                    if to is not None:
                        pairs.append((linear(x, core, y, z), linear(*to)))
    return pairs


def send(value, move):
    return lax.ppermute(value, ALL, pairs_of(move))


def contract(a, b, dim_a, dim_b):
    return lax.dot_general(
        a, b, (((dim_a,), (dim_b,)), ((), ())), precision=HI, preferred_element_type=jnp.float32
    )


def block_inverse(strips, group):
    lane = lax.broadcasted_iota(jnp.int32, (8, SB), 1)
    sublane = lax.broadcasted_iota(jnp.int32, (8, SB), 0)
    held = list(strips)
    count = len(held)
    for first in range(0, SB, group):
        own = first // 8
        columns = {}
        for t in range(own, count):
            columns[t] = [
                jnp.broadcast_to(held[t][:, first + m : first + m + 1], (8, SB)) for m in range(group)
            ]
        for m in range(group):
            r = first % 8 + m
            col = first + m
            tops = [jnp.broadcast_to(columns[own][k][r : r + 1, :], (8, SB)) for k in range(m, group)]
            inverse = 1.0 / tops[0]
            row = jnp.broadcast_to(held[own][r : r + 1, :], (8, SB))
            row = jnp.where(lane == col, 1.0, row)
            for t in range(own, count):
                scale = columns[t][m] * inverse
                if t == own:
                    if r == 7:
                        continue
                    scale = jnp.where(sublane > r, scale, 0.0)
                    held[t] = jnp.where((lane == col) & (sublane > r), -scale, held[t] - scale * row)
                else:
                    held[t] = jnp.where(lane == col, 0.0, held[t]) - scale * row
                for k in range(m + 1, group):
                    columns[t][k] = columns[t][k] - scale * tops[k - m]
    out = []
    for t in range(count):
        rows = sublane + 8 * t
        diagonal = jnp.sum(jnp.where(lane == rows, held[t], 0.0), axis=1, keepdims=True)
        unit = jnp.where(lane < rows, held[t], jnp.where(lane == rows, 1.0, 0.0))
        out.append(unit * lax.rsqrt(diagonal))
    return out


def pivot_kernel(parts_ref, inverse_ref, work, lower, diag):
    width = work.shape[0]
    half = width // 2
    left = parts_ref[0]
    right = parts_ref[1]
    work[...] = jnp.zeros_like(work)
    work[0:half, 0:half] = left[:, 0:half]
    work[half : half + SB, 0:half] = left[:, half : half + SB].T
    work[half:, half:] = right[:, 0:half]
    work[half + SB :, 0:SB] = right[0:SB, half:]
    work[half + SB :, SB:half] = right[SB:, half:]
    lower[...] = jnp.zeros_like(lower)
    inverse_ref[...] = jnp.zeros_like(inverse_ref)

    def step(k, carry):
        off = pl.multiple_of(k * SB, SB)
        strips = [work[pl.ds(off + 8 * t, 8), pl.ds(off, SB)] for t in range(SB // 8)]
        done = block_inverse(strips, 8)
        for t in range(SB // 8):
            diag[8 * t : 8 * t + 8, :] = done[t]
        inv = diag[...]
        below = contract(work[:, pl.ds(off, SB)], inv, 1, 1)
        rows = lax.broadcasted_iota(jnp.int32, (width, SB), 0)
        below = jnp.where(rows >= off + SB, below, 0.0)
        lower[:, pl.ds(off, SB)] = below
        work[...] = work[...] - contract(below, below, 1, 1)
        before = contract(lower[pl.ds(off, SB), :], inverse_ref[...], 1, 0)
        inverse_ref[pl.ds(off, SB), :] = -contract(inv, before, 1, 0)
        inverse_ref[pl.ds(off, SB), pl.ds(off, SB)] = inv
        return carry

    lax.fori_loop(0, width // SB, step, 0)


def pivot_inverse(parts):
    width = 2 * parts.shape[1]
    return pl.pallas_call(
        pivot_kernel,
        out_shape=jax.ShapeDtypeStruct((width, width), jnp.float32),
        scratch_shapes=[
            pltpu.VMEM((width, width), jnp.float32),
            pltpu.VMEM((width, width), jnp.float32),
            pltpu.VMEM((SB, SB), jnp.float32),
        ],
        compiler_params=pltpu.CompilerParams(vmem_limit_bytes=32 << 20),
    )(parts)


def solve_kernel(inverse_ref, panel_ref, window_ref, factor_ref, weight_ref):
    inverse = inverse_ref[...]
    factor_ref[...] = contract(panel_ref[...], inverse, 1, 1)
    weight_ref[...] = contract(contract(window_ref[...], inverse, 1, 1), inverse, 1, 0)


def solve(inverse, panel, window):
    shape = jax.ShapeDtypeStruct(panel.shape, jnp.float32)
    return pl.pallas_call(
        solve_kernel,
        out_shape=(shape, jax.ShapeDtypeStruct(window.shape, jnp.float32)),
        compiler_params=pltpu.CompilerParams(vmem_limit_bytes=32 << 20),
    )(inverse, panel, window)


def take_kernel(order, block_ref, out_ref):
    out_ref[...] = block_ref[...]


def take_blocks(order, blocks, size):
    count = order.shape[0]
    return pl.pallas_call(
        take_kernel,
        grid_spec=pltpu.PrefetchScalarGridSpec(
            num_scalar_prefetch=1,
            grid=(count,),
            in_specs=[pl.BlockSpec((size, size), lambda i, t: (t[i], 0))],
            out_specs=pl.BlockSpec((size, size), lambda i, t: (i, 0)),
        ),
        out_shape=jax.ShapeDtypeStruct((count * size, size), jnp.float32),
        compiler_params=pltpu.CompilerParams(vmem_limit_bytes=56 << 20),
    )(order, blocks)


BLOCK, OWN, OWN_HAS, FROM, FROM_HAS, PRESENT, ROWS = 0, 1, 2, (3, 4, 5), 6, 7, 8
NEAR = 4


def near_kernel(table, rows_ref, weight_ref, trailing_ref, own_ref, out_ref):
    i = pl.program_id(0)
    out_ref[...] = trailing_ref[...]

    @pl.when(table[OWN_HAS, i] == 1)
    def _():
        out_ref[...] += own_ref[...]

    @pl.when(table[PRESENT, i] == 1)
    def _():
        out_ref[...] -= contract(rows_ref[...], weight_ref[...], 1, 1)


def update_near(table, near, weight, trailing, own):
    size, width = weight.shape
    square = lambda pick: pl.BlockSpec((size, size), pick)
    return pl.pallas_call(
        near_kernel,
        grid_spec=pltpu.PrefetchScalarGridSpec(
            num_scalar_prefetch=1,
            grid=(NEAR,),
            in_specs=[
                pl.BlockSpec((size, width), lambda i, t: (t[ROWS, i], 0)),
                pl.BlockSpec((size, width), lambda i, t: (0, 0)),
                square(lambda i, t: (t[BLOCK, i], 0)),
                square(lambda i, t: (t[OWN, i], 0)),
            ],
            out_specs=square(lambda i, t: (t[BLOCK, i], 0)),
        ),
        out_shape=jax.ShapeDtypeStruct(trailing.shape, jnp.float32),
        compiler_params=pltpu.CompilerParams(vmem_limit_bytes=56 << 20),
    )(table, near, weight, trailing, own)


def far_kernel(table, done_ref, rows_ref, weight_ref, trailing_ref, own_ref, first_ref, main_ref, rest_ref, out_ref):
    i = pl.program_id(0)

    @pl.when(i < NEAR)
    def _():
        out_ref[...] = done_ref[...]

    @pl.when(i >= NEAR)
    def _():
        out_ref[...] = trailing_ref[...]

        @pl.when(table[OWN_HAS, i] == 1)
        def _():
            out_ref[...] += own_ref[...]

        @pl.when(table[PRESENT, i] == 1)
        def _():
            out_ref[...] -= contract(rows_ref[...], weight_ref[...], 1, 1)

    for number, other_ref in enumerate((first_ref, main_ref, rest_ref)):

        @pl.when(table[FROM_HAS, i] == number + 1)
        def _():
            out_ref[...] += other_ref[...]


def update_far(table, done, far, weight, trailing, own, others):
    size, width = weight.shape
    last = NEAR - 1
    square = lambda pick: pl.BlockSpec((size, size), pick)
    return pl.pallas_call(
        far_kernel,
        grid_spec=pltpu.PrefetchScalarGridSpec(
            num_scalar_prefetch=1,
            grid=(trailing.shape[0] // size,),
            in_specs=[
                square(lambda i, t: (t[BLOCK, jnp.minimum(i, last)], 0)),
                pl.BlockSpec((size, width), lambda i, t: (t[ROWS, jnp.maximum(i, NEAR)], 0)),
                pl.BlockSpec((size, width), lambda i, t: (0, 0)),
                square(lambda i, t: (t[BLOCK, jnp.maximum(i, NEAR)], 0)),
                square(lambda i, t: (t[OWN, jnp.maximum(i, NEAR)], 0)),
                *[square(lambda i, t, at=at: (t[at, i], 0)) for at in FROM],
            ],
            out_specs=square(lambda i, t: (t[BLOCK, i], 0)),
        ),
        out_shape=jax.ShapeDtypeStruct(trailing.shape, jnp.float32),
        input_output_aliases={1: 0},
        compiler_params=pltpu.CompilerParams(vmem_limit_bytes=56 << 20),
    )(table, done, far, weight, trailing, own, *others)


def kept(has, index):
    blocks = has.shape[0]
    coded = jnp.where(has, jnp.arange(blocks, dtype=jnp.int32) * blocks + index, -1)
    place = jnp.arange(blocks)
    latest = jnp.max(jnp.where(place[None, :] <= place[:, None], coded[None, :], -1), axis=1)
    return jnp.where(latest >= 0, latest % blocks, 0)


def lookup(slots, target):
    match = slots[None, :] == target[:, None]
    return jnp.any(match, axis=1), jnp.argmax(match, axis=1).astype(jnp.int32)


def crossing(slots, home, blocks):
    cross = slots // blocks != home
    k = jnp.arange(slots.shape[0])
    earlier = k[None, :] < k[:, None]
    ahead = jnp.sum(earlier & cross[None, :], axis=1)
    count = jnp.sum(cross)
    place = jnp.where(cross, ahead, count + k - ahead)
    order = jnp.sum(jnp.where(place[None, :] == k[:, None], k[None, :], 0), axis=1)
    return count, place.astype(jnp.int32), order.astype(jnp.int32)


STEPS = (("z", 4), ("z", 2), ("z", 1), ("y", 2), ("x", 2), ("x", 1))


def pivot_split(panel, core, y):
    half = panel.shape[1] // 2
    packed = jnp.concatenate([panel[SB:, 0:SB], panel[SB:, SB:half]], axis=0)
    from_left = panel[:, : half + SB]
    from_right = jnp.concatenate([panel[:, half:], packed], axis=1)
    whole = jnp.where(y == 0, from_left, from_right)
    split = send(
        whole[SB:], lambda x, c, y, z: (x, 1, y, z) if x == 0 and c == 0 and z == 0 and y < 2 else None
    )
    return jnp.where(core == 0, whole[:SB], split)


def pivot_spread(held, numbers, x, y, z):
    have = {(0, c, y, 0) for c in range(2) for y in range(2)}
    for number, (axis, stride) in enumerate(STEPS):
        targets = {}
        for place in sorted(have):
            to = list(place)
            to["xcyz".index(axis)] += stride
            targets[place] = tuple(to)
        have = have | set(targets.values())
        if number not in numbers:
            continue
        got = send(held, lambda x, c, y, z: targets.get((x, c, y, z)))
        coordinate = {"x": x, "y": y, "z": z}[axis]
        held = jnp.where((coordinate // stride) % 2 == 1, got, held)
    return held


def join_y(held, y):
    other = send(held, lambda x, c, y, z: (x, c, y ^ 1, z) if x == 0 else None)
    left = jnp.where(y % 2 == 0, held, other)
    right = jnp.where(y % 2 == 0, other, held)
    return jnp.stack([left, right])


def join_core(mine, core):
    theirs = send(mine, lambda x, c, y, z: (x, 1 - c, y, z))
    top = jnp.where(core == 0, mine, theirs)
    bottom = jnp.where(core == 0, theirs, mine)
    return jnp.concatenate([top, bottom], axis=1)


def window_owned(panel):
    place = {}
    for col in range(16):
        block = 2 + col
        place[(block // 16) * 16 + block % 16] = col
    return lax.ppermute(panel, ALL, sorted(place.items()))


def window_halves(held, z):
    got = send(held, lambda x, c, y, z: (x, c, y, z + 4) if x == 0 and c == 0 and z < 4 else None)
    return jnp.where(z >= 4, got, held)


def window_x(held, x, stride):
    got = send(
        held, lambda x, c, y, z: (x + stride, c, y, z) if x % (2 * stride) == 0 and c == 0 else None
    )
    return jnp.where((x // stride) % 2 == 1, got, held)


def window_core(held, core):
    got = send(held, lambda x, c, y, z: (x, 1, y, z) if c == 0 else None)
    return jnp.where(core == 1, got, held)


def gather_y(value):
    groups = [[zl * NY + y for y in range(NY)] for zl in range(NZ // 2)]
    return lax.all_gather(value, "col", axis_index_groups=groups, axis=0, tiled=True)


def swap(value):
    return send(value, lambda x, c, y, z: (x, c, y, (z + 4) % NZ))


def send_rest(order, child, size, both):
    first = swap(take_blocks(order[:1], child, size))
    second = lax.cond(
        both, lambda: swap(take_blocks(order[1:], child, size)), lambda: jnp.zeros_like(first)
    )
    return jnp.concatenate([first, second], axis=0)


def local(panel, trailing, child, child_map, pattern):
    size = trailing.shape[1]
    blocks = trailing.shape[0] // size
    sub = lax.axis_index("sub")
    row = lax.axis_index("row")
    col = lax.axis_index("col")
    x, core, y, z = row // 2, row % 2, col % NY, sub * 4 + col // NY
    own_slots = child_map[0]
    own_count, own_place, order = crossing(own_slots, sub, blocks)
    outgoing = [take_blocks(order[low:high], child[0], size) for low, high in ((0, FIRST), (FIRST, MAIN))]
    other_slots = swap(child_map)

    tie = lax.optimization_barrier
    zl = z % 4
    right = lambda value, at: send(value, lambda x, c, y, z: (x, c, y, z + 1) if z % 4 in at else None)
    left = lambda value, at: send(value, lambda x, c, y, z: (x, c, y, z - 1) if z % 4 in at else None)
    near = gather_y(panel)
    held = pivot_split(panel, core, y)
    window = window_owned(panel)
    held = pivot_spread(held, (0,), x, y, z)
    held, window, other_slots = tie((held, window, other_slots))
    other_slots = other_slots[0]
    window = window_halves(window, z)
    held = pivot_spread(held, (1,), x, y, z)

    other_count, other_place, _ = crossing(other_slots, 1 - sub, blocks)
    need = jnp.maximum(own_count, other_count)
    step = jnp.arange(blocks, dtype=jnp.int32)
    later = jnp.maximum(step - NEAR, 0)
    shift = jnp.where(step < NEAR, 0, 1 + later % 3)
    slots_z = jnp.array([[0, 1, 2, 3], [1, 2, 0, 3], [2, 3, 1, 0], [3, 2, 1, 0]], jnp.int32)[zl]
    step_z = jnp.sum(jnp.where(shift[:, None] == jnp.arange(4)[None, :], slots_z[None, :], 0), axis=1)
    block = step_z * NY + jnp.where(step < NEAR, step, later // 3)
    target = sub * blocks + block
    own_has, own_index = lookup(own_slots, target)
    other_has, other_index = lookup(other_slots, target)
    place = jnp.sum(
        jnp.where(other_index[:, None] == jnp.arange(other_place.shape[0])[None, :], other_place[None, :], 0),
        axis=1,
    )
    starts = (0, FIRST, MAIN)
    ends = (FIRST, MAIN, other_place.shape[0])
    inside = [other_has & (place >= low) & (place < high) for low, high in zip(starts, ends)]
    present = jnp.sum(jnp.where(block[:, None] == step[None, :], pattern[:, 0][None, :], 0), axis=1) == 1
    rows = jnp.concatenate([kept(present[:NEAR], step[:NEAR]), kept(present[NEAR:], later[NEAR:])])
    table = jnp.stack(
        [
            block,
            kept(own_has, own_index),
            own_has.astype(jnp.int32),
            *[kept(has, place - low) for has, low in zip(inside, starts)],
            sum((number + 1) * has.astype(jnp.int32) for number, has in enumerate(inside)),
            present.astype(jnp.int32),
            rows,
        ]
    ).astype(jnp.int32)

    held, table, need, outgoing = tie((held, table, need, outgoing))
    held = pivot_spread(held, (2,), x, y, z)
    held, window, bulk = tie((held, window, panel))
    from_left1, from_right1 = right(bulk, (0, 1, 2)), left(bulk, (1, 2, 3))
    held = pivot_spread(held, (3,), x, y, z)
    window = window_x(window, x, 2)
    held, from_left1, from_right1 = tie((held, from_left1, from_right1))
    from_left2, from_right2 = right(from_left1, (1, 2)), left(from_right1, (1, 2))
    held = join_y(held, y)
    held, from_left2, from_right2, near, window = tie((held, from_left2, from_right2, near, window))
    last = send(
        jnp.where(zl == 2, from_left2, from_right2),
        lambda x, c, y, z: {1: (x, c, y, z - 1), 2: (x, c, y, z + 1)}.get(z % 4),
    )
    held = pivot_spread(held, (4,), x, y, z)
    window = window_x(window, x, 1)
    held, last, window, outgoing = tie((held, last, window, outgoing))
    slot1 = jnp.where(zl == 3, from_left1, from_right1)
    slot2 = jnp.where(zl == 0, from_right2, jnp.where(zl == 3, from_left2, from_left1))
    slot3 = jnp.where(zl == 1, from_right2, jnp.where(zl == 2, from_left2, last))
    far = gather_y(jnp.concatenate([slot1, slot2, slot3], axis=0))
    first = swap(outgoing[0])
    main = swap(outgoing[1])
    window = window_core(window, core)
    held = pivot_spread(held, (5,), x, y, z)
    parts = join_core(held, core)
    inverse = pivot_inverse(parts)
    factor, weight = solve(inverse, panel, window)
    done = update_near(table, near, weight, trailing, child[0])
    done, main, need = tie((done, main, need))
    rest = lax.cond(
        need > MAIN,
        lambda: send_rest(order[MAIN:], child[0], size, need > MAIN + 1),
        lambda: jnp.zeros((2 * size, size), jnp.float32),
    )
    updated = update_far(table, done, far, weight, trailing, child[0], (first, main, rest))
    return (factor, updated)


def solution(mesh):
    return jax.shard_map(
        local,
        mesh=mesh,
        in_specs=(
            P(("sub", "row", "col"), None),
            P(("sub", "row"), "col"),
            P("sub", "row", "col"),
            P("sub", "row"),
            P(("sub", "row"), "col"),
        ),
        out_specs=(P(("sub", "row", "col"), None), P(("sub", "row"), "col")),
        check_vma=False,
    )
```

```python
import jax
import jax.numpy as jnp
from jax import lax
from jax.experimental import pallas as pl
from jax.experimental.pallas import tpu as pltpu
from jax.sharding import PartitionSpec as P

HI = lax.Precision.HIGHEST
ALL = ("sub", "row", "col")
SB = 128
NX, NY, NZ = 4, 4, 8
FIRST, MAIN = 1, 6


def linear(x, core, y, z):
    return (z // 4) * 128 + (x * 2 + core) * 16 + (z % 4) * 4 + y


def pairs_of(move):
    pairs = []
    for x in range(NX):
        for core in range(2):
            for y in range(NY):
                for z in range(NZ):
                    to = move(x, core, y, z)
                    if to is not None:
                        pairs.append((linear(x, core, y, z), linear(*to)))
    return pairs


def send(value, move):
    return lax.ppermute(value, ALL, pairs_of(move))


def contract(a, b, dim_a, dim_b):
    return lax.dot_general(
        a, b, (((dim_a,), (dim_b,)), ((), ())), precision=HI, preferred_element_type=jnp.float32
    )


def block_inverse(strips, group):
    lane = lax.broadcasted_iota(jnp.int32, (8, SB), 1)
    sublane = lax.broadcasted_iota(jnp.int32, (8, SB), 0)
    held = list(strips)
    count = len(held)
    for first in range(0, SB, group):
        own = first // 8
        columns = {}
        for t in range(own, count):
            columns[t] = [
                jnp.broadcast_to(held[t][:, first + m : first + m + 1], (8, SB)) for m in range(group)
            ]
        for m in range(group):
            r = first % 8 + m
            col = first + m
            tops = [jnp.broadcast_to(columns[own][k][r : r + 1, :], (8, SB)) for k in range(m, group)]
            inverse = 1.0 / tops[0]
            row = jnp.broadcast_to(held[own][r : r + 1, :], (8, SB))
            row = jnp.where(lane == col, 1.0, row)
            for t in range(own, count):
                scale = columns[t][m] * inverse
                if t == own:
                    if r == 7:
                        continue
                    scale = jnp.where(sublane > r, scale, 0.0)
                    held[t] = jnp.where((lane == col) & (sublane > r), -scale, held[t] - scale * row)
                else:
                    held[t] = jnp.where(lane == col, 0.0, held[t]) - scale * row
                for k in range(m + 1, group):
                    columns[t][k] = columns[t][k] - scale * tops[k - m]
    out = []
    for t in range(count):
        rows = sublane + 8 * t
        diagonal = jnp.sum(jnp.where(lane == rows, held[t], 0.0), axis=1, keepdims=True)
        unit = jnp.where(lane < rows, held[t], jnp.where(lane == rows, 1.0, 0.0))
        out.append(unit * lax.rsqrt(diagonal))
    return out


def pivot_kernel(parts_ref, inverse_ref, work, lower, diag):
    width = work.shape[0]
    half = width // 2
    left = parts_ref[0]
    right = parts_ref[1]
    work[...] = jnp.zeros_like(work)
    work[0:half, 0:half] = left[:, 0:half]
    work[half : half + SB, 0:half] = left[:, half : half + SB].T
    work[half:, half:] = right[:, 0:half]
    work[half + SB :, 0:SB] = right[0:SB, half:]
    work[half + SB :, SB:half] = right[SB:, half:]
    lower[...] = jnp.zeros_like(lower)
    inverse_ref[...] = jnp.zeros_like(inverse_ref)

    def step(k, carry):
        off = pl.multiple_of(k * SB, SB)
        strips = [work[pl.ds(off + 8 * t, 8), pl.ds(off, SB)] for t in range(SB // 8)]
        done = block_inverse(strips, 8)
        for t in range(SB // 8):
            diag[8 * t : 8 * t + 8, :] = done[t]
        inv = diag[...]
        below = contract(work[:, pl.ds(off, SB)], inv, 1, 1)
        rows = lax.broadcasted_iota(jnp.int32, (width, SB), 0)
        below = jnp.where(rows >= off + SB, below, 0.0)
        lower[:, pl.ds(off, SB)] = below
        work[...] = work[...] - contract(below, below, 1, 1)
        before = contract(lower[pl.ds(off, SB), :], inverse_ref[...], 1, 0)
        inverse_ref[pl.ds(off, SB), :] = -contract(inv, before, 1, 0)
        inverse_ref[pl.ds(off, SB), pl.ds(off, SB)] = inv
        return carry

    lax.fori_loop(0, width // SB, step, 0)


def pivot_inverse(parts):
    width = 2 * parts.shape[1]
    return pl.pallas_call(
        pivot_kernel,
        out_shape=jax.ShapeDtypeStruct((width, width), jnp.float32),
        scratch_shapes=[
            pltpu.VMEM((width, width), jnp.float32),
            pltpu.VMEM((width, width), jnp.float32),
            pltpu.VMEM((SB, SB), jnp.float32),
        ],
        compiler_params=pltpu.CompilerParams(vmem_limit_bytes=32 << 20),
    )(parts)


def solve_kernel(inverse_ref, panel_ref, window_ref, factor_ref, weight_ref):
    inverse = inverse_ref[...]
    factor_ref[...] = contract(panel_ref[...], inverse, 1, 1)
    weight_ref[...] = contract(contract(window_ref[...], inverse, 1, 1), inverse, 1, 0)


def solve(inverse, panel, window):
    shape = jax.ShapeDtypeStruct(panel.shape, jnp.float32)
    return pl.pallas_call(
        solve_kernel,
        out_shape=(shape, jax.ShapeDtypeStruct(window.shape, jnp.float32)),
        compiler_params=pltpu.CompilerParams(vmem_limit_bytes=32 << 20),
    )(inverse, panel, window)


def take_kernel(order, block_ref, out_ref):
    out_ref[...] = block_ref[...]


def take_blocks(order, blocks, size):
    count = order.shape[0]
    return pl.pallas_call(
        take_kernel,
        grid_spec=pltpu.PrefetchScalarGridSpec(
            num_scalar_prefetch=1,
            grid=(count,),
            in_specs=[pl.BlockSpec((size, size), lambda i, t: (t[i], 0))],
            out_specs=pl.BlockSpec((size, size), lambda i, t: (i, 0)),
        ),
        out_shape=jax.ShapeDtypeStruct((count * size, size), jnp.float32),
        compiler_params=pltpu.CompilerParams(vmem_limit_bytes=56 << 20),
    )(order, blocks)


BLOCK, OWN, OWN_HAS, FROM, FROM_HAS, PRESENT, ROWS = 0, 1, 2, (3, 4, 5), 6, 7, 8
NEAR = 4


def near_kernel(table, rows_ref, weight_ref, trailing_ref, own_ref, out_ref):
    i = pl.program_id(0)
    out_ref[...] = trailing_ref[...]

    @pl.when(table[OWN_HAS, i] == 1)
    def _():
        out_ref[...] += own_ref[...]

    @pl.when(table[PRESENT, i] == 1)
    def _():
        out_ref[...] -= contract(rows_ref[...], weight_ref[...], 1, 1)


def update_near(table, near, weight, trailing, own):
    size, width = weight.shape
    square = lambda pick: pl.BlockSpec((size, size), pick)
    return pl.pallas_call(
        near_kernel,
        grid_spec=pltpu.PrefetchScalarGridSpec(
            num_scalar_prefetch=1,
            grid=(NEAR,),
            in_specs=[
                pl.BlockSpec((size, width), lambda i, t: (t[ROWS, i], 0)),
                pl.BlockSpec((size, width), lambda i, t: (0, 0)),
                square(lambda i, t: (t[BLOCK, i], 0)),
                square(lambda i, t: (t[OWN, i], 0)),
            ],
            out_specs=square(lambda i, t: (t[BLOCK, i], 0)),
        ),
        out_shape=jax.ShapeDtypeStruct(trailing.shape, jnp.float32),
        compiler_params=pltpu.CompilerParams(vmem_limit_bytes=56 << 20),
    )(table, near, weight, trailing, own)


def far_kernel(table, done_ref, rows_ref, weight_ref, trailing_ref, own_ref, first_ref, main_ref, rest_ref, out_ref):
    i = pl.program_id(0)

    @pl.when(i < NEAR)
    def _():
        out_ref[...] = done_ref[...]

    @pl.when(i >= NEAR)
    def _():
        out_ref[...] = trailing_ref[...]

        @pl.when(table[OWN_HAS, i] == 1)
        def _():
            out_ref[...] += own_ref[...]

        @pl.when(table[PRESENT, i] == 1)
        def _():
            out_ref[...] -= contract(rows_ref[...], weight_ref[...], 1, 1)

    for number, other_ref in enumerate((first_ref, main_ref, rest_ref)):

        @pl.when(table[FROM_HAS, i] == number + 1)
        def _():
            out_ref[...] += other_ref[...]


def update_far(table, done, far, weight, trailing, own, others):
    size, width = weight.shape
    last = NEAR - 1
    square = lambda pick: pl.BlockSpec((size, size), pick)
    return pl.pallas_call(
        far_kernel,
        grid_spec=pltpu.PrefetchScalarGridSpec(
            num_scalar_prefetch=1,
            grid=(trailing.shape[0] // size,),
            in_specs=[
                square(lambda i, t: (t[BLOCK, jnp.minimum(i, last)], 0)),
                pl.BlockSpec((size, width), lambda i, t: (t[ROWS, jnp.maximum(i, NEAR)], 0)),
                pl.BlockSpec((size, width), lambda i, t: (0, 0)),
                square(lambda i, t: (t[BLOCK, jnp.maximum(i, NEAR)], 0)),
                square(lambda i, t: (t[OWN, jnp.maximum(i, NEAR)], 0)),
                *[square(lambda i, t, at=at: (t[at, i], 0)) for at in FROM],
            ],
            out_specs=square(lambda i, t: (t[BLOCK, i], 0)),
        ),
        out_shape=jax.ShapeDtypeStruct(trailing.shape, jnp.float32),
        input_output_aliases={1: 0},
        compiler_params=pltpu.CompilerParams(vmem_limit_bytes=56 << 20),
    )(table, done, far, weight, trailing, own, *others)


def kept(has, index):
    blocks = has.shape[0]
    coded = jnp.where(has, jnp.arange(blocks, dtype=jnp.int32) * blocks + index, -1)
    place = jnp.arange(blocks)
    latest = jnp.max(jnp.where(place[None, :] <= place[:, None], coded[None, :], -1), axis=1)
    return jnp.where(latest >= 0, latest % blocks, 0)


def lookup(slots, target):
    match = slots[None, :] == target[:, None]
    return jnp.any(match, axis=1), jnp.argmax(match, axis=1).astype(jnp.int32)


def crossing(slots, home, blocks):
    cross = slots // blocks != home
    k = jnp.arange(slots.shape[0])
    earlier = k[None, :] < k[:, None]
    ahead = jnp.sum(earlier & cross[None, :], axis=1)
    count = jnp.sum(cross)
    place = jnp.where(cross, ahead, count + k - ahead)
    order = jnp.sum(jnp.where(place[None, :] == k[:, None], k[None, :], 0), axis=1)
    return count, place.astype(jnp.int32), order.astype(jnp.int32)


STEPS = (("z", 4), ("z", 2), ("z", 1), ("y", 2), ("x", 2), ("x", 1))


def pivot_split(panel, core, y):
    half = panel.shape[1] // 2
    packed = jnp.concatenate([panel[SB:, 0:SB], panel[SB:, SB:half]], axis=0)
    from_left = panel[:, : half + SB]
    from_right = jnp.concatenate([panel[:, half:], packed], axis=1)
    whole = jnp.where(y == 0, from_left, from_right)
    split = send(
        whole[SB:], lambda x, c, y, z: (x, 1, y, z) if x == 0 and c == 0 and z == 0 and y < 2 else None
    )
    return jnp.where(core == 0, whole[:SB], split)


def pivot_spread(held, numbers, x, y, z):
    have = {(0, c, y, 0) for c in range(2) for y in range(2)}
    for number, (axis, stride) in enumerate(STEPS):
        targets = {}
        for place in sorted(have):
            to = list(place)
            to["xcyz".index(axis)] += stride
            targets[place] = tuple(to)
        have = have | set(targets.values())
        if number not in numbers:
            continue
        got = send(held, lambda x, c, y, z: targets.get((x, c, y, z)))
        coordinate = {"x": x, "y": y, "z": z}[axis]
        held = jnp.where((coordinate // stride) % 2 == 1, got, held)
    return held


def join_y(held, y):
    other = send(held, lambda x, c, y, z: (x, c, y ^ 1, z) if x == 0 else None)
    left = jnp.where(y % 2 == 0, held, other)
    right = jnp.where(y % 2 == 0, other, held)
    return jnp.stack([left, right])


def join_core(mine, core):
    theirs = send(mine, lambda x, c, y, z: (x, 1 - c, y, z))
    top = jnp.where(core == 0, mine, theirs)
    bottom = jnp.where(core == 0, theirs, mine)
    return jnp.concatenate([top, bottom], axis=1)


def window_owned(panel, half):
    place = {}
    for col in range(16):
        block = 2 + col
        place[(block // 16) * 16 + block % 16] = half * 128 + col
    return lax.ppermute(panel, ALL, sorted(place.items()))


def window_x(held, x, stride):
    got = send(
        held, lambda x, c, y, z: (x + stride, c, y, z) if x % (2 * stride) == 0 and c == 0 else None
    )
    return jnp.where((x // stride) % 2 == 1, got, held)


def window_core(held, core):
    got = send(held, lambda x, c, y, z: (x, 1, y, z) if c == 0 else None)
    return jnp.where(core == 1, got, held)


def gather_y(value):
    groups = [[zl * NY + y for y in range(NY)] for zl in range(NZ // 2)]
    return lax.all_gather(value, "col", axis_index_groups=groups, axis=0, tiled=True)


def swap(value):
    return send(value, lambda x, c, y, z: (x, c, y, (z + 4) % NZ))


def send_rest(order, child, size, both):
    first = swap(take_blocks(order[:1], child, size))
    second = lax.cond(
        both, lambda: swap(take_blocks(order[1:], child, size)), lambda: jnp.zeros_like(first)
    )
    return jnp.concatenate([first, second], axis=0)


def local(panel, trailing, child, child_map, pattern):
    size = trailing.shape[1]
    blocks = trailing.shape[0] // size
    sub = lax.axis_index("sub")
    row = lax.axis_index("row")
    col = lax.axis_index("col")
    x, core, y, z = row // 2, row % 2, col % NY, sub * 4 + col // NY
    tie = lax.optimization_barrier
    zl = z % 4
    right = lambda value, at: send(value, lambda x, c, y, z: (x, c, y, z + 1) if z % 4 in at else None)
    left = lambda value, at: send(value, lambda x, c, y, z: (x, c, y, z - 1) if z % 4 in at else None)
    near = gather_y(panel)
    held = pivot_split(panel, core, y)
    from_left1, from_right1 = right(panel, (0, 1, 2)), left(panel, (1, 2, 3))
    held, owned = tie((held, panel))
    windows = [window_owned(owned, half) for half in range(2)]
    held = pivot_spread(held, (0,), x, y, z)
    held, from_left1, from_right1, child_map = tie((held, from_left1, from_right1, child_map))
    own_slots = child_map[0]
    own_count, own_place, order = crossing(own_slots, sub, blocks)
    outgoing = [take_blocks(order[low:high], child[0], size) for low, high in ((0, FIRST), (FIRST, MAIN))]
    other_slots = swap(child_map)
    from_left2, from_right2 = right(from_left1, (1, 2)), left(from_right1, (1, 2))
    held = pivot_spread(held, (1,), x, y, z)
    held, from_left2, from_right2, other_slots = tie((held, from_left2, from_right2, other_slots))
    other_slots = other_slots[0]
    last = send(
        jnp.where(zl == 2, from_left2, from_right2),
        lambda x, c, y, z: {1: (x, c, y, z - 1), 2: (x, c, y, z + 1)}.get(z % 4),
    )
    held = pivot_spread(held, (2,), x, y, z)
    held, last, windows = tie((held, last, windows))
    window = jnp.where(z >= 4, windows[1], windows[0])
    window = window_x(window, x, 2)
    held = pivot_spread(held, (3,), x, y, z)

    other_count, other_place, _ = crossing(other_slots, 1 - sub, blocks)
    need = jnp.maximum(own_count, other_count)
    step = jnp.arange(blocks, dtype=jnp.int32)
    later = jnp.maximum(step - NEAR, 0)
    shift = jnp.where(step < NEAR, 0, 1 + later % 3)
    slots_z = jnp.array([[0, 1, 2, 3], [1, 2, 0, 3], [2, 3, 1, 0], [3, 2, 1, 0]], jnp.int32)[zl]
    step_z = jnp.sum(jnp.where(shift[:, None] == jnp.arange(4)[None, :], slots_z[None, :], 0), axis=1)
    block = step_z * NY + jnp.where(step < NEAR, step, later // 3)
    target = sub * blocks + block
    own_has, own_index = lookup(own_slots, target)
    other_has, other_index = lookup(other_slots, target)
    place = jnp.sum(
        jnp.where(other_index[:, None] == jnp.arange(other_place.shape[0])[None, :], other_place[None, :], 0),
        axis=1,
    )
    starts = (0, FIRST, MAIN)
    ends = (FIRST, MAIN, other_place.shape[0])
    inside = [other_has & (place >= low) & (place < high) for low, high in zip(starts, ends)]
    present = jnp.sum(jnp.where(block[:, None] == step[None, :], pattern[:, 0][None, :], 0), axis=1) == 1
    rows = jnp.concatenate([kept(present[:NEAR], step[:NEAR]), kept(present[NEAR:], later[NEAR:])])
    table = jnp.stack(
        [
            block,
            kept(own_has, own_index),
            own_has.astype(jnp.int32),
            *[kept(has, place - low) for has, low in zip(inside, starts)],
            sum((number + 1) * has.astype(jnp.int32) for number, has in enumerate(inside)),
            present.astype(jnp.int32),
            rows,
        ]
    ).astype(jnp.int32)

    slot1 = jnp.where(zl == 3, from_left1, from_right1)
    slot2 = jnp.where(zl == 0, from_right2, jnp.where(zl == 3, from_left2, from_left1))
    slot3 = jnp.where(zl == 1, from_right2, jnp.where(zl == 2, from_left2, last))
    slots = jnp.concatenate([slot1, slot2, slot3], axis=0)
    held, table, need, outgoing = tie((held, table, need, outgoing))
    first = swap(outgoing[0])
    held = join_y(held, y)
    held, near, window, slots = tie((held, near, window, slots))
    far = gather_y(slots)
    window = window_x(window, x, 1)
    held = pivot_spread(held, (4,), x, y, z)
    held, first, window, outgoing = tie((held, first, window, outgoing))
    main = swap(outgoing[1])
    window = window_core(window, core)
    held = pivot_spread(held, (5,), x, y, z)
    parts = join_core(held, core)
    inverse = pivot_inverse(parts)
    factor, weight = solve(inverse, panel, window)
    done = update_near(table, near, weight, trailing, child[0])
    done, main, need = tie((done, main, need))
    rest = lax.cond(
        need > MAIN,
        lambda: send_rest(order[MAIN:], child[0], size, need > MAIN + 1),
        lambda: jnp.zeros((2 * size, size), jnp.float32),
    )
    updated = update_far(table, done, far, weight, trailing, child[0], (first, main, rest))
    return (factor, updated)


def solution(mesh):
    return jax.shard_map(
        local,
        mesh=mesh,
        in_specs=(
            P(("sub", "row", "col"), None),
            P(("sub", "row"), "col"),
            P("sub", "row", "col"),
            P("sub", "row"),
            P(("sub", "row"), "col"),
        ),
        out_specs=(P(("sub", "row", "col"), None), P(("sub", "row"), "col")),
        check_vma=False,
    )
```

```python
import jax
import jax.numpy as jnp
from jax import lax
from jax.experimental import pallas as pl
from jax.experimental.pallas import tpu as pltpu
from jax.sharding import PartitionSpec as P

HI = lax.Precision.HIGHEST
ALL = ("sub", "row", "col")
SB = 128
NX, NY, NZ = 4, 4, 8
MAIN = 6


def linear(x, core, y, z):
    return (z // 4) * 128 + (x * 2 + core) * 16 + (z % 4) * 4 + y


def pairs_of(move):
    pairs = []
    for x in range(NX):
        for core in range(2):
            for y in range(NY):
                for z in range(NZ):
                    to = move(x, core, y, z)
                    if to is not None:
                        pairs.append((linear(x, core, y, z), linear(*to)))
    return pairs


def send(value, move):
    return lax.ppermute(value, ALL, pairs_of(move))


def contract(a, b, dim_a, dim_b):
    return lax.dot_general(
        a, b, (((dim_a,), (dim_b,)), ((), ())), precision=HI, preferred_element_type=jnp.float32
    )


def block_inverse(strips, group):
    lane = lax.broadcasted_iota(jnp.int32, (8, SB), 1)
    sublane = lax.broadcasted_iota(jnp.int32, (8, SB), 0)
    held = list(strips)
    count = len(held)
    for first in range(0, SB, group):
        own = first // 8
        columns = {}
        for t in range(own, count):
            columns[t] = [
                jnp.broadcast_to(held[t][:, first + m : first + m + 1], (8, SB)) for m in range(group)
            ]
        for m in range(group):
            r = first % 8 + m
            col = first + m
            tops = [jnp.broadcast_to(columns[own][k][r : r + 1, :], (8, SB)) for k in range(m, group)]
            inverse = 1.0 / tops[0]
            row = jnp.broadcast_to(held[own][r : r + 1, :], (8, SB))
            row = jnp.where(lane == col, 1.0, row)
            for t in range(own, count):
                scale = columns[t][m] * inverse
                if t == own:
                    if r == 7:
                        continue
                    scale = jnp.where(sublane > r, scale, 0.0)
                    held[t] = jnp.where((lane == col) & (sublane > r), -scale, held[t] - scale * row)
                else:
                    held[t] = jnp.where(lane == col, 0.0, held[t]) - scale * row
                for k in range(m + 1, group):
                    columns[t][k] = columns[t][k] - scale * tops[k - m]
    out = []
    for t in range(count):
        rows = sublane + 8 * t
        diagonal = jnp.sum(jnp.where(lane == rows, held[t], 0.0), axis=1, keepdims=True)
        unit = jnp.where(lane < rows, held[t], jnp.where(lane == rows, 1.0, 0.0))
        out.append(unit * lax.rsqrt(diagonal))
    return out


def pivot_kernel(parts_ref, inverse_ref, work, lower, diag):
    width = work.shape[0]
    half = width // 2
    left = parts_ref[0]
    right = parts_ref[1]
    work[...] = jnp.zeros_like(work)
    work[0:half, 0:half] = left[:, 0:half]
    work[half : half + SB, 0:half] = left[:, half : half + SB].T
    work[half:, half:] = right[:, 0:half]
    work[half + SB :, 0:SB] = right[0:SB, half:]
    work[half + SB :, SB:half] = right[SB:, half:]
    lower[...] = jnp.zeros_like(lower)
    inverse_ref[...] = jnp.zeros_like(inverse_ref)

    def step(k, carry):
        off = pl.multiple_of(k * SB, SB)
        strips = [work[pl.ds(off + 8 * t, 8), pl.ds(off, SB)] for t in range(SB // 8)]
        done = block_inverse(strips, 8)
        for t in range(SB // 8):
            diag[8 * t : 8 * t + 8, :] = done[t]
        inv = diag[...]
        below = contract(work[:, pl.ds(off, SB)], inv, 1, 1)
        rows = lax.broadcasted_iota(jnp.int32, (width, SB), 0)
        below = jnp.where(rows >= off + SB, below, 0.0)
        lower[:, pl.ds(off, SB)] = below
        work[...] = work[...] - contract(below, below, 1, 1)
        before = contract(lower[pl.ds(off, SB), :], inverse_ref[...], 1, 0)
        inverse_ref[pl.ds(off, SB), :] = -contract(inv, before, 1, 0)
        inverse_ref[pl.ds(off, SB), pl.ds(off, SB)] = inv
        return carry

    lax.fori_loop(0, width // SB, step, 0)


def pivot_inverse(parts):
    width = 2 * parts.shape[1]
    return pl.pallas_call(
        pivot_kernel,
        out_shape=jax.ShapeDtypeStruct((width, width), jnp.float32),
        scratch_shapes=[
            pltpu.VMEM((width, width), jnp.float32),
            pltpu.VMEM((width, width), jnp.float32),
            pltpu.VMEM((SB, SB), jnp.float32),
        ],
        compiler_params=pltpu.CompilerParams(vmem_limit_bytes=32 << 20),
    )(parts)


def thirds(value):
    first = value.astype(jnp.bfloat16)
    left = value - first.astype(jnp.float32)
    second = left.astype(jnp.bfloat16)
    return first, second, (left - second.astype(jnp.float32)).astype(jnp.bfloat16)


def product(rows, weights):
    a, b = thirds(rows), weights
    dot = lambda i, j: jnp.dot(a[i], b[j], preferred_element_type=jnp.float32)
    return dot(0, 0) + ((dot(0, 1) + dot(1, 0)) + ((dot(0, 2) + dot(1, 1)) + dot(2, 0)))


def solve_kernel(inverse_ref, panel_ref, window_ref, factor_ref, *weight_refs):
    inverse = inverse_ref[...]
    factor_ref[...] = contract(panel_ref[...], inverse, 1, 1)
    weight = contract(contract(window_ref[...], inverse, 1, 1), inverse, 1, 0)
    for weight_ref, value in zip(weight_refs, thirds(weight.T)):
        weight_ref[...] = value


def solve(inverse, panel, window):
    weight = jax.ShapeDtypeStruct((window.shape[1], window.shape[0]), jnp.bfloat16)
    factor, *weights = pl.pallas_call(
        solve_kernel,
        out_shape=(jax.ShapeDtypeStruct(panel.shape, jnp.float32), weight, weight, weight),
        compiler_params=pltpu.CompilerParams(vmem_limit_bytes=32 << 20),
    )(inverse, panel, window)
    return factor, weights


def take_kernel(order, block_ref, out_ref):
    out_ref[...] = block_ref[...]


def take_blocks(order, blocks, size):
    count = order.shape[0]
    return pl.pallas_call(
        take_kernel,
        grid_spec=pltpu.PrefetchScalarGridSpec(
            num_scalar_prefetch=1,
            grid=(count,),
            in_specs=[pl.BlockSpec((size, size), lambda i, t: (t[i], 0))],
            out_specs=pl.BlockSpec((size, size), lambda i, t: (i, 0)),
        ),
        out_shape=jax.ShapeDtypeStruct((count * size, size), jnp.float32),
        compiler_params=pltpu.CompilerParams(vmem_limit_bytes=56 << 20),
    )(order, blocks)


BLOCK, OWN, OWN_HAS, FROM, FROM_HAS, PRESENT, ROWS = 0, 1, 2, (3, 4), 5, 6, 7
NEAR = 4


def near_kernel(table, rows_ref, w0_ref, w1_ref, w2_ref, trailing_ref, own_ref, out_ref):
    i = pl.program_id(0)
    out_ref[...] = trailing_ref[...]

    @pl.when(table[OWN_HAS, i] == 1)
    def _():
        out_ref[...] += own_ref[...]

    @pl.when(table[PRESENT, i] == 1)
    def _():
        out_ref[...] -= product(rows_ref[...], (w0_ref[...], w1_ref[...], w2_ref[...]))


def update_near(table, near, weights, trailing, own):
    width, size = weights[0].shape
    square = lambda pick: pl.BlockSpec((size, size), pick)
    return pl.pallas_call(
        near_kernel,
        grid_spec=pltpu.PrefetchScalarGridSpec(
            num_scalar_prefetch=1,
            grid=(NEAR,),
            in_specs=[
                pl.BlockSpec((size, width), lambda i, t: (t[ROWS, i], 0)),
                *[pl.BlockSpec((width, size), lambda i, t: (0, 0)) for _ in weights],
                square(lambda i, t: (t[BLOCK, i], 0)),
                square(lambda i, t: (t[OWN, i], 0)),
            ],
            out_specs=square(lambda i, t: (t[BLOCK, i], 0)),
        ),
        out_shape=jax.ShapeDtypeStruct(trailing.shape, jnp.float32),
        compiler_params=pltpu.CompilerParams(vmem_limit_bytes=56 << 20),
    )(table, near, *weights, trailing, own)


def far_kernel(table, done_ref, rows_ref, w0_ref, w1_ref, w2_ref, trailing_ref, own_ref, main_ref, rest_ref, out_ref):
    i = pl.program_id(0)

    @pl.when(i < NEAR)
    def _():
        out_ref[...] = done_ref[...]

    @pl.when(i >= NEAR)
    def _():
        out_ref[...] = trailing_ref[...]

        @pl.when(table[OWN_HAS, i] == 1)
        def _():
            out_ref[...] += own_ref[...]

        @pl.when(table[PRESENT, i] == 1)
        def _():
            out_ref[...] -= product(rows_ref[...], (w0_ref[...], w1_ref[...], w2_ref[...]))

    for number, other_ref in enumerate((main_ref, rest_ref)):

        @pl.when(table[FROM_HAS, i] == number + 1)
        def _():
            out_ref[...] += other_ref[...]


def update_far(table, done, far, weights, trailing, own, others):
    width, size = weights[0].shape
    last = NEAR - 1
    square = lambda pick: pl.BlockSpec((size, size), pick)
    return pl.pallas_call(
        far_kernel,
        grid_spec=pltpu.PrefetchScalarGridSpec(
            num_scalar_prefetch=1,
            grid=(trailing.shape[0] // size,),
            in_specs=[
                square(lambda i, t: (t[BLOCK, jnp.minimum(i, last)], 0)),
                pl.BlockSpec((size, width), lambda i, t: (t[ROWS, jnp.maximum(i, NEAR)], 0)),
                *[pl.BlockSpec((width, size), lambda i, t: (0, 0)) for _ in weights],
                square(lambda i, t: (t[BLOCK, jnp.maximum(i, NEAR)], 0)),
                square(lambda i, t: (t[OWN, jnp.maximum(i, NEAR)], 0)),
                *[square(lambda i, t, at=at: (t[at, i], 0)) for at in FROM],
            ],
            out_specs=square(lambda i, t: (t[BLOCK, i], 0)),
        ),
        out_shape=jax.ShapeDtypeStruct(trailing.shape, jnp.float32),
        input_output_aliases={1: 0},
        compiler_params=pltpu.CompilerParams(vmem_limit_bytes=56 << 20),
    )(table, done, far, *weights, trailing, own, *others)


def kept(has, index):
    blocks = has.shape[0]
    coded = jnp.where(has, jnp.arange(blocks, dtype=jnp.int32) * blocks + index, -1)
    place = jnp.arange(blocks)
    latest = jnp.max(jnp.where(place[None, :] <= place[:, None], coded[None, :], -1), axis=1)
    return jnp.where(latest >= 0, latest % blocks, 0)


def lookup(slots, target):
    match = slots[None, :] == target[:, None]
    return jnp.any(match, axis=1), jnp.argmax(match, axis=1).astype(jnp.int32)


def crossing(slots, home, blocks):
    cross = slots // blocks != home
    k = jnp.arange(slots.shape[0])
    earlier = k[None, :] < k[:, None]
    ahead = jnp.sum(earlier & cross[None, :], axis=1)
    count = jnp.sum(cross)
    place = jnp.where(cross, ahead, count + k - ahead)
    order = jnp.sum(jnp.where(place[None, :] == k[:, None], k[None, :], 0), axis=1)
    return count, place.astype(jnp.int32), order.astype(jnp.int32)


STEPS = (("z", 4), ("z", 2), ("z", 1), ("y", 2), ("x", 2), ("x", 1))


def pivot_split(panel, core, y):
    half = panel.shape[1] // 2
    packed = jnp.concatenate([panel[SB:, 0:SB], panel[SB:, SB:half]], axis=0)
    from_left = panel[:, : half + SB]
    from_right = jnp.concatenate([panel[:, half:], packed], axis=1)
    whole = jnp.where(y == 0, from_left, from_right)
    split = send(
        whole[SB:], lambda x, c, y, z: (x, 1, y, z) if x == 0 and c == 0 and z == 0 and y < 2 else None
    )
    return jnp.where(core == 0, whole[:SB], split)


def pivot_spread(held, numbers, x, y, z):
    have = {(0, c, y, 0) for c in range(2) for y in range(2)}
    for number, (axis, stride) in enumerate(STEPS):
        targets = {}
        for place in sorted(have):
            to = list(place)
            to["xcyz".index(axis)] += stride
            targets[place] = tuple(to)
        have = have | set(targets.values())
        if number not in numbers:
            continue
        got = send(held, lambda x, c, y, z: targets.get((x, c, y, z)))
        coordinate = {"x": x, "y": y, "z": z}[axis]
        held = jnp.where((coordinate // stride) % 2 == 1, got, held)
    return held


def join_y(held, y):
    other = send(held, lambda x, c, y, z: (x, c, y ^ 1, z) if x == 0 else None)
    left = jnp.where(y % 2 == 0, held, other)
    right = jnp.where(y % 2 == 0, other, held)
    return jnp.stack([left, right])


def join_core(mine, core):
    theirs = send(mine, lambda x, c, y, z: (x, 1 - c, y, z))
    top = jnp.where(core == 0, mine, theirs)
    bottom = jnp.where(core == 0, theirs, mine)
    return jnp.concatenate([top, bottom], axis=1)


def window_owned(panel, half):
    place = {}
    for col in range(16):
        block = 2 + col
        place[(block // 16) * 16 + block % 16] = half * 128 + col
    return lax.ppermute(panel, ALL, sorted(place.items()))


def window_x(held, x, stride):
    got = send(
        held, lambda x, c, y, z: (x + stride, c, y, z) if x % (2 * stride) == 0 and c == 0 else None
    )
    return jnp.where((x // stride) % 2 == 1, got, held)


def window_core(held, core):
    got = send(held, lambda x, c, y, z: (x, 1, y, z) if c == 0 else None)
    return jnp.where(core == 1, got, held)


def gather_y(value):
    groups = [[zl * NY + y for y in range(NY)] for zl in range(NZ // 2)]
    return lax.all_gather(value, "col", axis_index_groups=groups, axis=0, tiled=True)


def swap(value):
    return send(value, lambda x, c, y, z: (x, c, y, (z + 4) % NZ))


def send_rest(order, child, size, both):
    first = swap(take_blocks(order[:1], child, size))
    second = lax.cond(
        both, lambda: swap(take_blocks(order[1:], child, size)), lambda: jnp.zeros_like(first)
    )
    return jnp.concatenate([first, second], axis=0)


def local(panel, trailing, child, child_map, pattern):
    size = trailing.shape[1]
    blocks = trailing.shape[0] // size
    sub = lax.axis_index("sub")
    row = lax.axis_index("row")
    col = lax.axis_index("col")
    x, core, y, z = row // 2, row % 2, col % NY, sub * 4 + col // NY
    tie = lax.optimization_barrier
    zl = z % 4
    right = lambda value, at: send(value, lambda x, c, y, z: (x, c, y, z + 1) if z % 4 in at else None)
    left = lambda value, at: send(value, lambda x, c, y, z: (x, c, y, z - 1) if z % 4 in at else None)
    near = gather_y(panel)
    held = pivot_split(panel, core, y)
    from_left1, from_right1 = right(panel, (0, 1, 2)), left(panel, (1, 2, 3))
    held, owned = tie((held, panel))
    windows = [window_owned(owned, half) for half in range(2)]
    held = pivot_spread(held, (0,), x, y, z)
    held, from_left1, from_right1, child_map = tie((held, from_left1, from_right1, child_map))
    own_slots = child_map[0]
    own_count, own_place, order = crossing(own_slots, sub, blocks)
    outgoing = take_blocks(order[:MAIN], child[0], size)
    other_slots = swap(child_map)
    from_left2, from_right2 = right(from_left1, (1, 2)), left(from_right1, (1, 2))
    held = pivot_spread(held, (1,), x, y, z)
    held, from_left2, from_right2, other_slots = tie((held, from_left2, from_right2, other_slots))
    other_slots = other_slots[0]
    last = send(
        jnp.where(zl == 2, from_left2, from_right2),
        lambda x, c, y, z: {1: (x, c, y, z - 1), 2: (x, c, y, z + 1)}.get(z % 4),
    )
    held = pivot_spread(held, (2,), x, y, z)
    held, last, windows = tie((held, last, windows))
    window = jnp.where(z >= 4, windows[1], windows[0])
    window = window_x(window, x, 2)
    held = pivot_spread(held, (3,), x, y, z)

    other_count, other_place, _ = crossing(other_slots, 1 - sub, blocks)
    need = jnp.maximum(own_count, other_count)
    step = jnp.arange(blocks, dtype=jnp.int32)
    later = jnp.maximum(step - NEAR, 0)
    shift = jnp.where(step < NEAR, 0, 1 + later % 3)
    slots_z = jnp.array([[0, 1, 2, 3], [1, 2, 0, 3], [2, 3, 1, 0], [3, 2, 1, 0]], jnp.int32)[zl]
    step_z = jnp.sum(jnp.where(shift[:, None] == jnp.arange(4)[None, :], slots_z[None, :], 0), axis=1)
    block = step_z * NY + jnp.where(step < NEAR, step, later // 3)
    target = sub * blocks + block
    own_has, own_index = lookup(own_slots, target)
    other_has, other_index = lookup(other_slots, target)
    place = jnp.sum(
        jnp.where(other_index[:, None] == jnp.arange(other_place.shape[0])[None, :], other_place[None, :], 0),
        axis=1,
    )
    starts = (0, MAIN)
    ends = (MAIN, other_place.shape[0])
    inside = [other_has & (place >= low) & (place < high) for low, high in zip(starts, ends)]
    present = jnp.sum(jnp.where(block[:, None] == step[None, :], pattern[:, 0][None, :], 0), axis=1) == 1
    rows = jnp.concatenate([kept(present[:NEAR], step[:NEAR]), kept(present[NEAR:], later[NEAR:])])
    table = jnp.stack(
        [
            block,
            kept(own_has, own_index),
            own_has.astype(jnp.int32),
            *[kept(has, place - low) for has, low in zip(inside, starts)],
            sum((number + 1) * has.astype(jnp.int32) for number, has in enumerate(inside)),
            present.astype(jnp.int32),
            rows,
        ]
    ).astype(jnp.int32)

    slot1 = jnp.where(zl == 3, from_left1, from_right1)
    slot2 = jnp.where(zl == 0, from_right2, jnp.where(zl == 3, from_left2, from_left1))
    slot3 = jnp.where(zl == 1, from_right2, jnp.where(zl == 2, from_left2, last))
    slots = jnp.concatenate([slot1, slot2, slot3], axis=0)
    held, table, need, outgoing = tie((held, table, need, outgoing))
    main = swap(outgoing)
    held = join_y(held, y)
    held, near, window, slots = tie((held, near, window, slots))
    far = gather_y(slots)
    window = window_x(window, x, 1)
    held = pivot_spread(held, (4,), x, y, z)
    held, window = tie((held, window))
    window = window_core(window, core)
    held = pivot_spread(held, (5,), x, y, z)
    parts = join_core(held, core)
    inverse = pivot_inverse(parts)
    factor, weights = solve(inverse, panel, window)
    done = update_near(table, near, weights, trailing, child[0])
    done, main, need = tie((done, main, need))
    rest = lax.cond(
        need > MAIN,
        lambda: send_rest(order[MAIN:], child[0], size, need > MAIN + 1),
        lambda: jnp.zeros((2 * size, size), jnp.float32),
    )
    updated = update_far(table, done, far, weights, trailing, child[0], (main, rest))
    return (factor, updated)


def solution(mesh):
    return jax.shard_map(
        local,
        mesh=mesh,
        in_specs=(
            P(("sub", "row", "col"), None),
            P(("sub", "row"), "col"),
            P("sub", "row", "col"),
            P("sub", "row"),
            P(("sub", "row"), "col"),
        ),
        out_specs=(P(("sub", "row", "col"), None), P(("sub", "row"), "col")),
        check_vma=False,
    )
```

```python
import jax
import jax.numpy as jnp
from jax import lax
from jax.experimental import pallas as pl
from jax.experimental.pallas import tpu as pltpu
from jax.sharding import PartitionSpec as P

HI = lax.Precision.HIGHEST
ALL = ("sub", "row", "col")
SB = 128
NX, NY, NZ = 4, 4, 8
MAIN = 6


def linear(x, core, y, z):
    return (z // 4) * 128 + (x * 2 + core) * 16 + (z % 4) * 4 + y


def pairs_of(move):
    pairs = []
    for x in range(NX):
        for core in range(2):
            for y in range(NY):
                for z in range(NZ):
                    to = move(x, core, y, z)
                    if to is not None:
                        pairs.append((linear(x, core, y, z), linear(*to)))
    return pairs


def send(value, move):
    return lax.ppermute(value, ALL, pairs_of(move))


def contract(a, b, dim_a, dim_b):
    return lax.dot_general(
        a, b, (((dim_a,), (dim_b,)), ((), ())), precision=HI, preferred_element_type=jnp.float32
    )


def block_inverse(strips, group):
    lane = lax.broadcasted_iota(jnp.int32, (8, SB), 1)
    sublane = lax.broadcasted_iota(jnp.int32, (8, SB), 0)
    held = list(strips)
    count = len(held)
    for first in range(0, SB, group):
        own = first // 8
        columns = {}
        for t in range(own, count):
            columns[t] = [
                jnp.broadcast_to(held[t][:, first + m : first + m + 1], (8, SB)) for m in range(group)
            ]
        for m in range(group):
            r = first % 8 + m
            col = first + m
            tops = [jnp.broadcast_to(columns[own][k][r : r + 1, :], (8, SB)) for k in range(m, group)]
            inverse = 1.0 / tops[0]
            row = jnp.broadcast_to(held[own][r : r + 1, :], (8, SB))
            row = jnp.where(lane == col, 1.0, row)
            for t in range(own, count):
                scale = columns[t][m] * inverse
                if t == own:
                    if r == 7:
                        continue
                    scale = jnp.where(sublane > r, scale, 0.0)
                    held[t] = jnp.where((lane == col) & (sublane > r), -scale, held[t] - scale * row)
                else:
                    held[t] = jnp.where(lane == col, 0.0, held[t]) - scale * row
                for k in range(m + 1, group):
                    columns[t][k] = columns[t][k] - scale * tops[k - m]
    out = []
    for t in range(count):
        rows = sublane + 8 * t
        diagonal = jnp.sum(jnp.where(lane == rows, held[t], 0.0), axis=1, keepdims=True)
        unit = jnp.where(lane < rows, held[t], jnp.where(lane == rows, 1.0, 0.0))
        out.append(unit * lax.rsqrt(diagonal))
    return out


def pivot_kernel(parts_ref, inverse_ref, work, lower, diag):
    width = work.shape[0]
    half = width // 2
    left = parts_ref[0]
    right = parts_ref[1]
    work[...] = jnp.zeros_like(work)
    work[0:half, 0:half] = left[:, 0:half]
    work[half : half + SB, 0:half] = left[:, half : half + SB].T
    work[half:, half:] = right[:, 0:half]
    work[half + SB :, 0:SB] = right[0:SB, half:]
    work[half + SB :, SB:half] = right[SB:, half:]
    lower[...] = jnp.zeros_like(lower)
    inverse_ref[...] = jnp.zeros_like(inverse_ref)

    def step(k, carry):
        off = pl.multiple_of(k * SB, SB)
        strips = [work[pl.ds(off + 8 * t, 8), pl.ds(off, SB)] for t in range(SB // 8)]
        done = block_inverse(strips, 8)
        for t in range(SB // 8):
            diag[8 * t : 8 * t + 8, :] = done[t]
        inv = diag[...]
        below = contract(work[:, pl.ds(off, SB)], inv, 1, 1)
        rows = lax.broadcasted_iota(jnp.int32, (width, SB), 0)
        below = jnp.where(rows >= off + SB, below, 0.0)
        lower[:, pl.ds(off, SB)] = below
        work[...] = work[...] - contract(below, below, 1, 1)
        before = contract(lower[pl.ds(off, SB), :], inverse_ref[...], 1, 0)
        inverse_ref[pl.ds(off, SB), :] = -contract(inv, before, 1, 0)
        inverse_ref[pl.ds(off, SB), pl.ds(off, SB)] = inv
        return carry

    lax.fori_loop(0, width // SB, step, 0)


def pivot_inverse(parts):
    width = 2 * parts.shape[1]
    return pl.pallas_call(
        pivot_kernel,
        out_shape=jax.ShapeDtypeStruct((width, width), jnp.float32),
        scratch_shapes=[
            pltpu.VMEM((width, width), jnp.float32),
            pltpu.VMEM((width, width), jnp.float32),
            pltpu.VMEM((SB, SB), jnp.float32),
        ],
        compiler_params=pltpu.CompilerParams(vmem_limit_bytes=32 << 20),
    )(parts)


def thirds(value):
    first = value.astype(jnp.bfloat16)
    left = value - first.astype(jnp.float32)
    second = left.astype(jnp.bfloat16)
    return first, second, (left - second.astype(jnp.float32)).astype(jnp.bfloat16)


def product(rows, weights):
    a, b = thirds(rows), weights
    dot = lambda i, j: jnp.dot(a[i], b[j], preferred_element_type=jnp.float32)
    return dot(0, 0) + ((dot(0, 1) + dot(1, 0)) + ((dot(0, 2) + dot(1, 1)) + dot(2, 0)))


def solve_kernel(inverse_ref, panel_ref, window_ref, factor_ref, *weight_refs):
    inverse = inverse_ref[...]
    factor_ref[...] = contract(panel_ref[...], inverse, 1, 1)
    weight = contract(contract(window_ref[...], inverse, 1, 1), inverse, 1, 0)
    for weight_ref, value in zip(weight_refs, thirds(weight.T)):
        weight_ref[...] = value


def solve(inverse, panel, window):
    weight = jax.ShapeDtypeStruct((window.shape[1], window.shape[0]), jnp.bfloat16)
    factor, *weights = pl.pallas_call(
        solve_kernel,
        out_shape=(jax.ShapeDtypeStruct(panel.shape, jnp.float32), weight, weight, weight),
        compiler_params=pltpu.CompilerParams(vmem_limit_bytes=32 << 20),
    )(inverse, panel, window)
    return factor, weights


def take_kernel(order, block_ref, out_ref):
    out_ref[...] = block_ref[...]


def take_blocks(order, blocks, size):
    count = order.shape[0]
    return pl.pallas_call(
        take_kernel,
        grid_spec=pltpu.PrefetchScalarGridSpec(
            num_scalar_prefetch=1,
            grid=(count,),
            in_specs=[pl.BlockSpec((size, size), lambda i, t: (t[i], 0))],
            out_specs=pl.BlockSpec((size, size), lambda i, t: (i, 0)),
        ),
        out_shape=jax.ShapeDtypeStruct((count * size, size), jnp.float32),
        compiler_params=pltpu.CompilerParams(vmem_limit_bytes=56 << 20),
    )(order, blocks)


BLOCK, OWN, OWN_HAS, FROM, FROM_HAS, PRESENT, ROWS = 0, 1, 2, (3, 4), 5, 6, 7
NEAR = 4


def update_kernel(
    table, w0_ref, w1_ref, w2_ref, near, far, trailing, own, main, rest, out,
    rows, base, own_held, main_held, rest_held, rows_sem, base_sem, child_sem, out_sem,
):
    blocks, size = base.shape[:2]
    place = lambda i: pl.ds(pl.multiple_of(table[BLOCK, i] * size, size), size)
    children = [
        pltpu.make_async_copy(source, held, child_sem.at[k])
        for k, (source, held) in enumerate(((own, own_held), (main, main_held), (rest, rest_held)))
    ]
    rows_in = lambda i: pltpu.make_async_copy(
        near.at[pl.ds(i * size, size)] if i < NEAR else far.at[pl.ds((i - NEAR) * size, size)],
        rows.at[i],
        rows_sem.at[i],
    )
    base_in = lambda i: pltpu.make_async_copy(trailing.at[place(i)], base.at[i], base_sem.at[i])
    base_out = lambda i: pltpu.make_async_copy(base.at[i], out.at[place(i)], out_sem.at[i])
    for copy in children:
        copy.start()
    for i in range(blocks):
        base_in(i).start()

        @pl.when(table[PRESENT, i] == 1)
        def _(i=i):
            rows_in(i).start()

    for copy in children:
        copy.wait()
    for i in range(blocks):
        base_in(i).wait()
        for has, at, held in (
            (table[OWN_HAS, i] == 1, OWN, own_held),
            (table[FROM_HAS, i] == 1, FROM[0], main_held),
            (table[FROM_HAS, i] == 2, FROM[1], rest_held),
        ):

            @pl.when(has)
            def _(at=at, held=held):
                base[i] += held[pl.ds(pl.multiple_of(table[at, i] * size, size), size), :]

        @pl.when(table[PRESENT, i] == 1)
        def _(i=i):
            rows_in(i).wait()
            base[i] -= product(rows[i], (w0_ref[...], w1_ref[...], w2_ref[...]))

        base_out(i).start()
    for i in range(blocks):
        base_out(i).wait()


def update(table, near, far, weights, trailing, own, main, rest):
    width, size = weights[0].shape
    blocks = trailing.shape[0] // size
    anywhere = pl.BlockSpec(memory_space=pl.ANY)
    inside = pl.BlockSpec(memory_space=pltpu.VMEM)
    return pl.pallas_call(
        update_kernel,
        in_specs=[pl.BlockSpec(memory_space=pltpu.SMEM), inside, inside, inside] + [anywhere] * 6,
        out_specs=anywhere,
        out_shape=jax.ShapeDtypeStruct(trailing.shape, jnp.float32),
        scratch_shapes=[
            pltpu.VMEM((blocks, size, width), jnp.float32),
            pltpu.VMEM((blocks, size, size), jnp.float32),
            pltpu.VMEM(own.shape, jnp.float32),
            pltpu.VMEM(main.shape, jnp.float32),
            pltpu.VMEM(rest.shape, jnp.float32),
            pltpu.SemaphoreType.DMA((blocks,)),
            pltpu.SemaphoreType.DMA((blocks,)),
            pltpu.SemaphoreType.DMA((3,)),
            pltpu.SemaphoreType.DMA((blocks,)),
        ],
        compiler_params=pltpu.CompilerParams(vmem_limit_bytes=56 << 20),
    )(table, *weights, near, far, trailing, own, main, rest)


def kept(has, index):
    blocks = has.shape[0]
    coded = jnp.where(has, jnp.arange(blocks, dtype=jnp.int32) * blocks + index, -1)
    place = jnp.arange(blocks)
    latest = jnp.max(jnp.where(place[None, :] <= place[:, None], coded[None, :], -1), axis=1)
    return jnp.where(latest >= 0, latest % blocks, 0)


def lookup(slots, target):
    match = slots[None, :] == target[:, None]
    return jnp.any(match, axis=1), jnp.argmax(match, axis=1).astype(jnp.int32)


def crossing(slots, home, blocks):
    cross = slots // blocks != home
    k = jnp.arange(slots.shape[0])
    earlier = k[None, :] < k[:, None]
    ahead = jnp.sum(earlier & cross[None, :], axis=1)
    count = jnp.sum(cross)
    place = jnp.where(cross, ahead, count + k - ahead)
    order = jnp.sum(jnp.where(place[None, :] == k[:, None], k[None, :], 0), axis=1)
    return count, place.astype(jnp.int32), order.astype(jnp.int32)


STEPS = (("z", 4), ("z", 2), ("z", 1), ("y", 2), ("x", 2), ("x", 1))


def pivot_split(panel, core, y):
    half = panel.shape[1] // 2
    packed = jnp.concatenate([panel[SB:, 0:SB], panel[SB:, SB:half]], axis=0)
    from_left = panel[:, : half + SB]
    from_right = jnp.concatenate([panel[:, half:], packed], axis=1)
    whole = jnp.where(y == 0, from_left, from_right)
    split = send(
        whole[SB:], lambda x, c, y, z: (x, 1, y, z) if x == 0 and c == 0 and z == 0 and y < 2 else None
    )
    return jnp.where(core == 0, whole[:SB], split)


def pivot_spread(held, numbers, x, y, z):
    have = {(0, c, y, 0) for c in range(2) for y in range(2)}
    for number, (axis, stride) in enumerate(STEPS):
        targets = {}
        for place in sorted(have):
            to = list(place)
            to["xcyz".index(axis)] += stride
            targets[place] = tuple(to)
        have = have | set(targets.values())
        if number not in numbers:
            continue
        got = send(held, lambda x, c, y, z: targets.get((x, c, y, z)))
        coordinate = {"x": x, "y": y, "z": z}[axis]
        held = jnp.where((coordinate // stride) % 2 == 1, got, held)
    return held


def join_y(held, y):
    other = send(held, lambda x, c, y, z: (x, c, y ^ 1, z) if x == 0 else None)
    left = jnp.where(y % 2 == 0, held, other)
    right = jnp.where(y % 2 == 0, other, held)
    return jnp.stack([left, right])


def join_core(mine, core):
    theirs = send(mine, lambda x, c, y, z: (x, 1 - c, y, z))
    top = jnp.where(core == 0, mine, theirs)
    bottom = jnp.where(core == 0, theirs, mine)
    return jnp.concatenate([top, bottom], axis=1)


def window_owned(panel, half):
    place = {}
    for col in range(16):
        block = 2 + col
        place[(block // 16) * 16 + block % 16] = half * 128 + col
    return lax.ppermute(panel, ALL, sorted(place.items()))


def window_x(held, x, stride):
    got = send(
        held, lambda x, c, y, z: (x + stride, c, y, z) if x % (2 * stride) == 0 and c == 0 else None
    )
    return jnp.where((x // stride) % 2 == 1, got, held)


def window_core(held, core):
    got = send(held, lambda x, c, y, z: (x, 1, y, z) if c == 0 else None)
    return jnp.where(core == 1, got, held)


def gather_y(value):
    groups = [[zl * NY + y for y in range(NY)] for zl in range(NZ // 2)]
    return lax.all_gather(value, "col", axis_index_groups=groups, axis=0, tiled=True)


def swap(value):
    return send(value, lambda x, c, y, z: (x, c, y, (z + 4) % NZ))


def send_rest(order, child, size, both):
    first = swap(take_blocks(order[:1], child, size))
    second = lax.cond(
        both, lambda: swap(take_blocks(order[1:], child, size)), lambda: jnp.zeros_like(first)
    )
    return jnp.concatenate([first, second], axis=0)


def local(panel, trailing, child, child_map, pattern):
    size = trailing.shape[1]
    blocks = trailing.shape[0] // size
    sub = lax.axis_index("sub")
    row = lax.axis_index("row")
    col = lax.axis_index("col")
    x, core, y, z = row // 2, row % 2, col % NY, sub * 4 + col // NY
    tie = lax.optimization_barrier
    zl = z % 4
    right = lambda value, at: send(value, lambda x, c, y, z: (x, c, y, z + 1) if z % 4 in at else None)
    left = lambda value, at: send(value, lambda x, c, y, z: (x, c, y, z - 1) if z % 4 in at else None)
    near = gather_y(panel)
    held = pivot_split(panel, core, y)
    from_left1, from_right1 = right(panel, (0, 1, 2)), left(panel, (1, 2, 3))
    held, owned = tie((held, panel))
    windows = [window_owned(owned, half) for half in range(2)]
    held = pivot_spread(held, (0,), x, y, z)
    held, from_left1, from_right1, child_map = tie((held, from_left1, from_right1, child_map))
    own_slots = child_map[0]
    own_count, own_place, order = crossing(own_slots, sub, blocks)
    outgoing = take_blocks(order[:MAIN], child[0], size)
    other_slots = swap(child_map)
    from_left2, from_right2 = right(from_left1, (1, 2)), left(from_right1, (1, 2))
    held = pivot_spread(held, (1,), x, y, z)
    held, from_left2, from_right2, other_slots = tie((held, from_left2, from_right2, other_slots))
    other_slots = other_slots[0]
    last = send(
        jnp.where(zl == 2, from_left2, from_right2),
        lambda x, c, y, z: {1: (x, c, y, z - 1), 2: (x, c, y, z + 1)}.get(z % 4),
    )
    held = pivot_spread(held, (2,), x, y, z)
    held, last, windows = tie((held, last, windows))
    window = jnp.where(z >= 4, windows[1], windows[0])
    window = window_x(window, x, 2)
    held = pivot_spread(held, (3,), x, y, z)

    other_count, other_place, _ = crossing(other_slots, 1 - sub, blocks)
    need = jnp.maximum(own_count, other_count)
    step = jnp.arange(blocks, dtype=jnp.int32)
    later = jnp.maximum(step - NEAR, 0)
    shift = jnp.where(step < NEAR, 0, 1 + later % 3)
    slots_z = jnp.array([[0, 1, 2, 3], [1, 2, 0, 3], [2, 3, 1, 0], [3, 2, 1, 0]], jnp.int32)[zl]
    step_z = jnp.sum(jnp.where(shift[:, None] == jnp.arange(4)[None, :], slots_z[None, :], 0), axis=1)
    block = step_z * NY + jnp.where(step < NEAR, step, later // 3)
    target = sub * blocks + block
    own_has, own_index = lookup(own_slots, target)
    other_has, other_index = lookup(other_slots, target)
    place = jnp.sum(
        jnp.where(other_index[:, None] == jnp.arange(other_place.shape[0])[None, :], other_place[None, :], 0),
        axis=1,
    )
    starts = (0, MAIN)
    ends = (MAIN, other_place.shape[0])
    inside = [other_has & (place >= low) & (place < high) for low, high in zip(starts, ends)]
    present = jnp.sum(jnp.where(block[:, None] == step[None, :], pattern[:, 0][None, :], 0), axis=1) == 1
    rows = jnp.concatenate([kept(present[:NEAR], step[:NEAR]), kept(present[NEAR:], later[NEAR:])])
    table = jnp.stack(
        [
            block,
            kept(own_has, own_index),
            own_has.astype(jnp.int32),
            *[kept(has, place - low) for has, low in zip(inside, starts)],
            sum((number + 1) * has.astype(jnp.int32) for number, has in enumerate(inside)),
            present.astype(jnp.int32),
            rows,
        ]
    ).astype(jnp.int32)

    slot1 = jnp.where(zl == 3, from_left1, from_right1)
    slot2 = jnp.where(zl == 0, from_right2, jnp.where(zl == 3, from_left2, from_left1))
    slot3 = jnp.where(zl == 1, from_right2, jnp.where(zl == 2, from_left2, last))
    slots = jnp.concatenate([slot1, slot2, slot3], axis=0)
    held, table, need, outgoing = tie((held, table, need, outgoing))
    main = swap(outgoing)
    held = join_y(held, y)
    held, near, window, slots = tie((held, near, window, slots))
    far = gather_y(slots)
    window = window_x(window, x, 1)
    held = pivot_spread(held, (4,), x, y, z)
    held, window = tie((held, window))
    window = window_core(window, core)
    held = pivot_spread(held, (5,), x, y, z)
    parts = join_core(held, core)
    inverse = pivot_inverse(parts)
    factor, weights = solve(inverse, panel, window)
    weights, main, need = tie((weights, main, need))
    rest = lax.cond(
        need > MAIN,
        lambda: send_rest(order[MAIN:], child[0], size, need > MAIN + 1),
        lambda: jnp.zeros((2 * size, size), jnp.float32),
    )
    updated = update(table, near, far, weights, trailing, child[0], main, rest)
    return (factor, updated)


def solution(mesh):
    return jax.shard_map(
        local,
        mesh=mesh,
        in_specs=(
            P(("sub", "row", "col"), None),
            P(("sub", "row"), "col"),
            P("sub", "row", "col"),
            P("sub", "row"),
            P(("sub", "row"), "col"),
        ),
        out_specs=(P(("sub", "row", "col"), None), P(("sub", "row"), "col")),
        check_vma=False,
    )
```

```python
import jax
import jax.numpy as jnp
from jax import lax
from jax.experimental import pallas as pl
from jax.experimental.pallas import tpu as pltpu
from jax.sharding import PartitionSpec as P

HI = lax.Precision.HIGHEST
ALL = ("sub", "row", "col")
SB = 128
NX, NY, NZ = 4, 4, 8
MAIN = 6


def linear(x, core, y, z):
    return (z // 4) * 128 + (x * 2 + core) * 16 + (z % 4) * 4 + y


def pairs_of(move):
    pairs = []
    for x in range(NX):
        for core in range(2):
            for y in range(NY):
                for z in range(NZ):
                    to = move(x, core, y, z)
                    if to is not None:
                        pairs.append((linear(x, core, y, z), linear(*to)))
    return pairs


def send(value, move):
    return lax.ppermute(value, ALL, pairs_of(move))


def contract(a, b, dim_a, dim_b):
    return lax.dot_general(
        a, b, (((dim_a,), (dim_b,)), ((), ())), precision=HI, preferred_element_type=jnp.float32
    )


def block_inverse(strips, group):
    lane = lax.broadcasted_iota(jnp.int32, (8, SB), 1)
    sublane = lax.broadcasted_iota(jnp.int32, (8, SB), 0)
    held = list(strips)
    count = len(held)
    for first in range(0, SB, group):
        own = first // 8
        columns = {}
        for t in range(own, count):
            columns[t] = [
                jnp.broadcast_to(held[t][:, first + m : first + m + 1], (8, SB)) for m in range(group)
            ]
        for m in range(group):
            r = first % 8 + m
            col = first + m
            tops = [jnp.broadcast_to(columns[own][k][r : r + 1, :], (8, SB)) for k in range(m, group)]
            inverse = 1.0 / tops[0]
            row = jnp.broadcast_to(held[own][r : r + 1, :], (8, SB))
            row = jnp.where(lane == col, 1.0, row)
            for t in range(own, count):
                scale = columns[t][m] * inverse
                if t == own:
                    if r == 7:
                        continue
                    scale = jnp.where(sublane > r, scale, 0.0)
                    held[t] = jnp.where((lane == col) & (sublane > r), -scale, held[t] - scale * row)
                else:
                    held[t] = jnp.where(lane == col, 0.0, held[t]) - scale * row
                for k in range(m + 1, group):
                    columns[t][k] = columns[t][k] - scale * tops[k - m]
    out = []
    for t in range(count):
        rows = sublane + 8 * t
        diagonal = jnp.sum(jnp.where(lane == rows, held[t], 0.0), axis=1, keepdims=True)
        unit = jnp.where(lane < rows, held[t], jnp.where(lane == rows, 1.0, 0.0))
        out.append(unit * lax.rsqrt(diagonal))
    return out


def pivot_kernel(parts_ref, inverse_ref, work, lower, diag):
    width = work.shape[0]
    half = width // 2
    left = parts_ref[0]
    right = parts_ref[1]
    work[...] = jnp.zeros_like(work)
    work[0:half, 0:half] = left[:, 0:half]
    work[half : half + SB, 0:half] = left[:, half : half + SB].T
    work[half:, half:] = right[:, 0:half]
    work[half + SB :, 0:SB] = right[0:SB, half:]
    work[half + SB :, SB:half] = right[SB:, half:]
    lower[...] = jnp.zeros_like(lower)
    inverse_ref[...] = jnp.zeros_like(inverse_ref)

    def step(k, carry):
        off = pl.multiple_of(k * SB, SB)
        strips = [work[pl.ds(off + 8 * t, 8), pl.ds(off, SB)] for t in range(SB // 8)]
        done = block_inverse(strips, 8)
        for t in range(SB // 8):
            diag[8 * t : 8 * t + 8, :] = done[t]
        inv = diag[...]
        below = contract(work[:, pl.ds(off, SB)], inv, 1, 1)
        rows = lax.broadcasted_iota(jnp.int32, (width, SB), 0)
        below = jnp.where(rows >= off + SB, below, 0.0)
        lower[:, pl.ds(off, SB)] = below
        work[...] = work[...] - contract(below, below, 1, 1)
        before = contract(lower[pl.ds(off, SB), :], inverse_ref[...], 1, 0)
        inverse_ref[pl.ds(off, SB), :] = -contract(inv, before, 1, 0)
        inverse_ref[pl.ds(off, SB), pl.ds(off, SB)] = inv
        return carry

    lax.fori_loop(0, width // SB, step, 0)


def pivot_inverse(parts):
    width = 2 * parts.shape[1]
    return pl.pallas_call(
        pivot_kernel,
        out_shape=jax.ShapeDtypeStruct((width, width), jnp.float32),
        scratch_shapes=[
            pltpu.VMEM((width, width), jnp.float32),
            pltpu.VMEM((width, width), jnp.float32),
            pltpu.VMEM((SB, SB), jnp.float32),
        ],
        compiler_params=pltpu.CompilerParams(vmem_limit_bytes=32 << 20),
    )(parts)


def thirds(value):
    first = value.astype(jnp.bfloat16)
    left = value - first.astype(jnp.float32)
    second = left.astype(jnp.bfloat16)
    return first, second, (left - second.astype(jnp.float32)).astype(jnp.bfloat16)


def product(rows, weights):
    a, b = thirds(rows), weights
    dot = lambda i, j: jnp.dot(a[i], b[j], preferred_element_type=jnp.float32)
    return dot(0, 0) + ((dot(0, 1) + dot(1, 0)) + ((dot(0, 2) + dot(1, 1)) + dot(2, 0)))


def solve_kernel(inverse_ref, panel_ref, window_ref, factor_ref, *weight_refs):
    inverse = inverse_ref[...]
    factor_ref[...] = contract(panel_ref[...], inverse, 1, 1)
    weight = contract(contract(window_ref[...], inverse, 1, 1), inverse, 1, 0)
    for weight_ref, value in zip(weight_refs, thirds(weight.T)):
        weight_ref[...] = value


def solve(inverse, panel, window):
    weight = jax.ShapeDtypeStruct((window.shape[1], window.shape[0]), jnp.bfloat16)
    factor, *weights = pl.pallas_call(
        solve_kernel,
        out_shape=(jax.ShapeDtypeStruct(panel.shape, jnp.float32), weight, weight, weight),
        compiler_params=pltpu.CompilerParams(vmem_limit_bytes=32 << 20),
    )(inverse, panel, window)
    return factor, weights


def take_kernel(order, block_ref, out_ref):
    out_ref[...] = block_ref[...]


def take_blocks(order, blocks, size):
    count = order.shape[0]
    return pl.pallas_call(
        take_kernel,
        grid_spec=pltpu.PrefetchScalarGridSpec(
            num_scalar_prefetch=1,
            grid=(count,),
            in_specs=[pl.BlockSpec((size, size), lambda i, t: (t[i], 0))],
            out_specs=pl.BlockSpec((size, size), lambda i, t: (i, 0)),
        ),
        out_shape=jax.ShapeDtypeStruct((count * size, size), jnp.float32),
        compiler_params=pltpu.CompilerParams(vmem_limit_bytes=56 << 20),
    )(order, blocks)


BLOCK, OWN, OWN_HAS, FROM, FROM_HAS, PRESENT, ROWS = 0, 1, 2, (3, 4), 5, 6, 7
NEAR = 4


def update_kernel(
    table, w0_ref, w1_ref, w2_ref, near, far, trailing, own, main, rest, out,
    rows, base, own_held, main_held, rest_held, rows_sem, base_sem, child_sem, out_sem,
):
    blocks, size = base.shape[:2]
    place = lambda i: pl.ds(pl.multiple_of(table[BLOCK, i] * size, size), size)
    children = [
        pltpu.make_async_copy(source, held, child_sem.at[k])
        for k, (source, held) in enumerate(((own, own_held), (main, main_held), (rest, rest_held)))
    ]
    rows_in = lambda i: pltpu.make_async_copy(
        near.at[pl.ds(i * size, size)] if i < NEAR else far.at[pl.ds((i - NEAR) * size, size)],
        rows.at[i],
        rows_sem.at[i],
    )
    base_in = lambda i: pltpu.make_async_copy(trailing.at[place(i)], base.at[i], base_sem.at[i])
    base_out = lambda i: pltpu.make_async_copy(base.at[i], out.at[place(i)], out_sem.at[i])
    for copy in children:
        copy.start()
    for i in range(blocks):
        base_in(i).start()

        @pl.when(table[PRESENT, i] == 1)
        def _(i=i):
            rows_in(i).start()

    for copy in children:
        copy.wait()
    for i in range(blocks):
        base_in(i).wait()
        for has, at, held in (
            (table[OWN_HAS, i] == 1, OWN, own_held),
            (table[FROM_HAS, i] == 1, FROM[0], main_held),
            (table[FROM_HAS, i] == 2, FROM[1], rest_held),
        ):

            @pl.when(has)
            def _(at=at, held=held):
                base[i] += held[pl.ds(pl.multiple_of(table[at, i] * size, size), size), :]

        @pl.when(table[PRESENT, i] == 1)
        def _(i=i):
            rows_in(i).wait()
            base[i] -= product(rows[i], (w0_ref[...], w1_ref[...], w2_ref[...]))

        base_out(i).start()
    for i in range(blocks):
        base_out(i).wait()


def update(table, near, far, weights, trailing, own, main, rest):
    width, size = weights[0].shape
    blocks = trailing.shape[0] // size
    anywhere = pl.BlockSpec(memory_space=pl.ANY)
    inside = pl.BlockSpec(memory_space=pltpu.VMEM)
    return pl.pallas_call(
        update_kernel,
        in_specs=[pl.BlockSpec(memory_space=pltpu.SMEM), inside, inside, inside] + [anywhere] * 6,
        out_specs=anywhere,
        out_shape=jax.ShapeDtypeStruct(trailing.shape, jnp.float32),
        scratch_shapes=[
            pltpu.VMEM((blocks, size, width), jnp.float32),
            pltpu.VMEM((blocks, size, size), jnp.float32),
            pltpu.VMEM(own.shape, jnp.float32),
            pltpu.VMEM(main.shape, jnp.float32),
            pltpu.VMEM(rest.shape, jnp.float32),
            pltpu.SemaphoreType.DMA((blocks,)),
            pltpu.SemaphoreType.DMA((blocks,)),
            pltpu.SemaphoreType.DMA((3,)),
            pltpu.SemaphoreType.DMA((blocks,)),
        ],
        compiler_params=pltpu.CompilerParams(vmem_limit_bytes=56 << 20),
    )(table, *weights, near, far, trailing, own, main, rest)


def kept(has, index):
    blocks = has.shape[0]
    coded = jnp.where(has, jnp.arange(blocks, dtype=jnp.int32) * blocks + index, -1)
    place = jnp.arange(blocks)
    latest = jnp.max(jnp.where(place[None, :] <= place[:, None], coded[None, :], -1), axis=1)
    return jnp.where(latest >= 0, latest % blocks, 0)


def lookup(slots, target):
    match = slots[None, :] == target[:, None]
    return jnp.any(match, axis=1), jnp.argmax(match, axis=1).astype(jnp.int32)


def crossing(slots, home, blocks):
    cross = slots // blocks != home
    k = jnp.arange(slots.shape[0])
    earlier = k[None, :] < k[:, None]
    ahead = jnp.sum(earlier & cross[None, :], axis=1)
    count = jnp.sum(cross)
    place = jnp.where(cross, ahead, count + k - ahead)
    order = jnp.sum(jnp.where(place[None, :] == k[:, None], k[None, :], 0), axis=1)
    return count, place.astype(jnp.int32), order.astype(jnp.int32)


STEPS = (("z", 4), ("z", 2), ("z", 1), ("y", 2), ("x", 2), ("x", 1))


def pivot_split(panel, core, y):
    half = panel.shape[1] // 2
    packed = jnp.concatenate([panel[SB:, 0:SB], panel[SB:, SB:half]], axis=0)
    from_left = panel[:, : half + SB]
    from_right = jnp.concatenate([panel[:, half:], packed], axis=1)
    whole = jnp.where(y == 0, from_left, from_right)
    split = send(
        whole[SB:], lambda x, c, y, z: (x, 1, y, z) if x == 0 and c == 0 and z == 0 and y < 2 else None
    )
    return jnp.where(core == 0, whole[:SB], split)


def pivot_spread(held, numbers, x, y, z):
    have = {(0, c, y, 0) for c in range(2) for y in range(2)}
    for number, (axis, stride) in enumerate(STEPS):
        targets = {}
        for place in sorted(have):
            to = list(place)
            to["xcyz".index(axis)] += stride
            targets[place] = tuple(to)
        have = have | set(targets.values())
        if number not in numbers:
            continue
        got = send(held, lambda x, c, y, z: targets.get((x, c, y, z)))
        coordinate = {"x": x, "y": y, "z": z}[axis]
        held = jnp.where((coordinate // stride) % 2 == 1, got, held)
    return held


def join_y(held, y):
    other = send(held, lambda x, c, y, z: (x, c, y ^ 1, z) if x == 0 else None)
    left = jnp.where(y % 2 == 0, held, other)
    right = jnp.where(y % 2 == 0, other, held)
    return jnp.stack([left, right])


def join_core(mine, core):
    theirs = send(mine, lambda x, c, y, z: (x, 1 - c, y, z))
    top = jnp.where(core == 0, mine, theirs)
    bottom = jnp.where(core == 0, theirs, mine)
    return jnp.concatenate([top, bottom], axis=1)


def window_owned(panel, half):
    place = {}
    for col in range(16):
        block = 2 + col
        place[(block // 16) * 16 + block % 16] = half * 128 + col
    return lax.ppermute(panel, ALL, sorted(place.items()))


def window_x(held, x, stride):
    got = send(
        held, lambda x, c, y, z: (x + stride, c, y, z) if x % (2 * stride) == 0 and c == 0 else None
    )
    return jnp.where((x // stride) % 2 == 1, got, held)


def window_core(held, core):
    got = send(held, lambda x, c, y, z: (x, 1, y, z) if c == 0 else None)
    return jnp.where(core == 1, got, held)


def gather_y(value):
    groups = [[zl * NY + y for y in range(NY)] for zl in range(NZ // 2)]
    return lax.all_gather(value, "col", axis_index_groups=groups, axis=0, tiled=True)


def swap(value):
    return send(value, lambda x, c, y, z: (x, c, y, (z + 4) % NZ))


def send_rest(order, child, size, both):
    first = swap(take_blocks(order[:1], child, size))
    second = lax.cond(
        both, lambda: swap(take_blocks(order[1:], child, size)), lambda: jnp.zeros_like(first)
    )
    return jnp.concatenate([first, second], axis=0)


def local(panel, trailing, child, child_map, pattern):
    size = trailing.shape[1]
    blocks = trailing.shape[0] // size
    sub = lax.axis_index("sub")
    row = lax.axis_index("row")
    col = lax.axis_index("col")
    x, core, y, z = row // 2, row % 2, col % NY, sub * 4 + col // NY
    tie = lax.optimization_barrier
    zl = z % 4
    right = lambda value, at: send(value, lambda x, c, y, z: (x, c, y, z + 1) if z % 4 in at else None)
    left = lambda value, at: send(value, lambda x, c, y, z: (x, c, y, z - 1) if z % 4 in at else None)
    near = gather_y(panel)
    held = pivot_split(panel, core, y)
    from_left1, from_right1 = right(panel, (0, 1, 2)), left(panel, (1, 2, 3))
    held, owned = tie((held, panel))
    windows = [window_owned(owned, half) for half in range(2)]
    held = pivot_spread(held, (0,), x, y, z)
    held, from_left1, from_right1, child_map = tie((held, from_left1, from_right1, child_map))
    own_slots = child_map[0]
    own_count, own_place, order = crossing(own_slots, sub, blocks)
    outgoing = take_blocks(order[:MAIN], child[0], size)
    other_slots = swap(child_map)
    from_left2, from_right2 = right(from_left1, (1, 2)), left(from_right1, (1, 2))
    held = pivot_spread(held, (1,), x, y, z)
    held, from_left2, from_right2, other_slots = tie((held, from_left2, from_right2, other_slots))
    other_slots = other_slots[0]
    last = send(
        jnp.where(zl == 2, from_left2, from_right2),
        lambda x, c, y, z: {1: (x, c, y, z - 1), 2: (x, c, y, z + 1)}.get(z % 4),
    )
    held = pivot_spread(held, (2,), x, y, z)
    held, last, windows = tie((held, last, windows))
    window = jnp.where(z >= 4, windows[1], windows[0])
    window = window_x(window, x, 2)
    held = pivot_spread(held, (3,), x, y, z)

    other_count, other_place, _ = crossing(other_slots, 1 - sub, blocks)
    need = jnp.maximum(own_count, other_count)
    step = jnp.arange(blocks, dtype=jnp.int32)
    later = jnp.maximum(step - NEAR, 0)
    shift = jnp.where(step < NEAR, 0, 1 + later % 3)
    slots_z = jnp.array([[0, 1, 2, 3], [1, 2, 0, 3], [2, 3, 1, 0], [3, 2, 1, 0]], jnp.int32)[zl]
    step_z = jnp.sum(jnp.where(shift[:, None] == jnp.arange(4)[None, :], slots_z[None, :], 0), axis=1)
    block = step_z * NY + jnp.where(step < NEAR, step, later // 3)
    target = sub * blocks + block
    own_has, own_index = lookup(own_slots, target)
    other_has, other_index = lookup(other_slots, target)
    place = jnp.sum(
        jnp.where(other_index[:, None] == jnp.arange(other_place.shape[0])[None, :], other_place[None, :], 0),
        axis=1,
    )
    starts = (0, MAIN)
    ends = (MAIN, other_place.shape[0])
    inside = [other_has & (place >= low) & (place < high) for low, high in zip(starts, ends)]
    present = jnp.sum(jnp.where(block[:, None] == step[None, :], pattern[:, 0][None, :], 0), axis=1) == 1
    rows = jnp.concatenate([kept(present[:NEAR], step[:NEAR]), kept(present[NEAR:], later[NEAR:])])
    table = jnp.stack(
        [
            block,
            kept(own_has, own_index),
            own_has.astype(jnp.int32),
            *[kept(has, place - low) for has, low in zip(inside, starts)],
            sum((number + 1) * has.astype(jnp.int32) for number, has in enumerate(inside)),
            present.astype(jnp.int32),
            rows,
        ]
    ).astype(jnp.int32)

    slot1 = jnp.where(zl == 3, from_left1, from_right1)
    slot2 = jnp.where(zl == 0, from_right2, jnp.where(zl == 3, from_left2, from_left1))
    slot3 = jnp.where(zl == 1, from_right2, jnp.where(zl == 2, from_left2, last))
    slots = jnp.concatenate([slot1, slot2, slot3], axis=0)
    held, table, need, outgoing = tie((held, table, need, outgoing))
    main = swap(outgoing)
    held = join_y(held, y)
    held, near, window, slots = tie((held, near, window, slots))
    far = gather_y(slots)
    window = window_x(window, x, 1)
    held = pivot_spread(held, (4,), x, y, z)
    held = pivot_spread(held, (5,), x, y, z)
    window = window_core(window, core)
    parts = join_core(held, core)
    inverse = pivot_inverse(parts)
    factor, weights = solve(inverse, panel, window)
    weights, main, need = tie((weights, main, need))
    rest = lax.cond(
        need > MAIN,
        lambda: send_rest(order[MAIN:], child[0], size, need > MAIN + 1),
        lambda: jnp.zeros((2 * size, size), jnp.float32),
    )
    updated = update(table, near, far, weights, trailing, child[0], main, rest)
    return (factor, updated)


def solution(mesh):
    return jax.shard_map(
        local,
        mesh=mesh,
        in_specs=(
            P(("sub", "row", "col"), None),
            P(("sub", "row"), "col"),
            P("sub", "row", "col"),
            P("sub", "row"),
            P(("sub", "row"), "col"),
        ),
        out_specs=(P(("sub", "row", "col"), None), P(("sub", "row"), "col")),
        check_vma=False,
    )
```
